512 devices in a mesh: seq: 128 (over y, z, core), head: 4 (over x).
Axes of the slice: x: 4, y: 4, z: 16, core: 2. Of those that a mesh axis runs over, the one named last changes fastest.
Arguments:
- query_rows: bfloat16 [16384, 2048], P('seq', 'head'), may hold values from -5 to 5
- key_rows: bfloat16 [16384, 2048], P('seq', 'head'), may hold values from -5 to 5
- value_rows: bfloat16 [16384, 2048], P('seq', 'head'), may hold values from -6 to 6
- out_weight: bfloat16 [2048, 2048], P('head'), may hold values from -0.125 to 0.125
Outputs:
- layer_output: bfloat16 [16384, 2048], P(('seq', 'head'))
The draws below stay inside these ranges and needn't reach their ends.
All inputs are finite; a program needn't handle non-finite values.
Results may differ from the reference program's by a relative error of at most 0.0053.
Values may be sent and summed in bfloat16 or wider, within the bound.
A program may use at most 128 MiB of HBM per device.

```python
import math
import jax
import jax.numpy as jnp
from jax import lax

D = 2048
HEADS = 16
HEAD_DIM = 128
SEG0 = 1024
LEVELS = 5
TOKENS = 16384


def draw_query_rows(key, part):
    key = jax.random.fold_in(key, 1)
    values = jnp.clip(jax.random.normal(key, (TOKENS, HEADS * HEAD_DIM), jnp.float32), -5.0, 5.0)
    return values.astype(jnp.bfloat16)


def draw_key_rows(key, part):
    key = jax.random.fold_in(key, 2)
    values = jnp.clip(jax.random.normal(key, (TOKENS, HEADS * HEAD_DIM), jnp.float32), -5.0, 5.0)
    return values.astype(jnp.bfloat16)


def block_levels(key, shape, shards, low, top_value):
    loudness, own = 1.0, jax.random.fold_in(key, 6)
    for position, shards_of in shards:
        draws = jnp.exp(jax.random.uniform(jax.random.fold_in(own, position), (shards_of,), jnp.float32, low / len(shards), top_value / len(shards)))
        loudness = loudness * jnp.repeat(draws, shape[position] // shards_of).reshape([-1 if axis == position else 1 for axis in range(len(shape))])
    return loudness


def normal_values(key, dims, scale, limit, shards=(), kind=jnp.bfloat16):
    drawn = jax.random.normal(key, dims, jnp.float32) * scale
    if len(shards) > 0:
        drawn = block_levels(key, dims, shards, -0.22, 0.18) * drawn
    return jnp.clip(drawn, min=-limit, max=limit).astype(kind)


def setup_inputs(seed: int = 0) -> dict:
    key_list = jax.random.split(jax.random.key(seed), 5)
    return {
        "query_rows": draw_query_rows(jax.random.fold_in(key_list[4], 71), 0),
        "key_rows": draw_key_rows(jax.random.fold_in(key_list[4], 71), 0),
        "value_rows": normal_values(key_list[2], (TOKENS, HEADS * HEAD_DIM), 1.0, 6.0, ((0, 128), (1, 4))),
        "out_weight": normal_values(key_list[3], (HEADS * HEAD_DIM, D), (HEADS * HEAD_DIM) ** -0.5, 0.125, ((0, 4),)),
    }


very_low = -1e+30

def segment_parts(q_seg, k_seg, v_seg):
    score_scale = 1.0 / math.sqrt(HEAD_DIM)
    scores = jnp.dot(q_seg, k_seg.T, preferred_element_type=jnp.float32) * score_scale
    count_rows = q_seg.shape[0]
    allowed = jnp.arange(count_rows)[None, :] <= jnp.arange(count_rows)[:, None]
    masked = jnp.where(allowed, scores, very_low)
    peak_score = lax.optimization_barrier(jnp.max(masked, axis=1))
    weights = jnp.where(allowed, jnp.exp(masked - peak_score[:, None]), 0.0)
    denominator = lax.optimization_barrier(jnp.sum(weights, axis=1))
    numerator = jnp.dot(weights.astype(jnp.bfloat16), v_seg, preferred_element_type=jnp.float32)
    return (peak_score, denominator, numerator)

def reference(query_rows, key_rows, value_rows, out_weight):
    head_outputs = []
    for head_index in range(HEADS):
        lower = head_index * HEAD_DIM
        q_head = query_rows[:, lower:lower + HEAD_DIM]
        k_head = key_rows[:, lower:lower + HEAD_DIM]
        v_head = value_rows[:, lower:lower + HEAD_DIM]
        for level_index in range(LEVELS):
            step_rate = 2 ** level_index
            span_len = min(SEG0 * step_rate, TOKENS)
            segment_len = span_len // step_rate
            segments = TOKENS // span_len
            offset_now = head_index % step_rate

            def pick_rows(array):
                return array.reshape(segments, segment_len, step_rate, HEAD_DIM)[:, :, offset_now]
            peak_score, denominator, numerator = lax.map(lambda triple: segment_parts(triple[0], triple[1], triple[2]), (pick_rows(q_head), pick_rows(k_head), pick_rows(v_head)))
            full_peak = jnp.full((segments, segment_len, step_rate), very_low, jnp.float32)
            full_peak = full_peak.at[:, :, offset_now].set(peak_score).reshape(TOKENS)
            full_denom = jnp.zeros((segments, segment_len, step_rate), jnp.float32)
            full_denom = full_denom.at[:, :, offset_now].set(denominator).reshape(TOKENS)
            full_numer = jnp.zeros((segments, segment_len, step_rate, HEAD_DIM), jnp.float32)
            full_numer = full_numer.at[:, :, offset_now].set(numerator).reshape(TOKENS, HEAD_DIM)
            if level_index == 0:
                run_peak, run_denom, run_numer = (full_peak, full_denom, full_numer)
            else:
                new_peak = jnp.maximum(run_peak, full_peak)
                old_factor = jnp.exp(run_peak - new_peak)
                new_factor = jnp.exp(full_peak - new_peak)
                run_denom = run_denom * old_factor + full_denom * new_factor
                run_numer = run_numer * old_factor[:, None] + full_numer * new_factor[:, None]
                run_peak = new_peak
        head_outputs.append((run_numer / run_denom[:, None]).astype(jnp.bfloat16))
    attention = jnp.concatenate(head_outputs, axis=1)
    return jnp.dot(attention, out_weight, preferred_element_type=jnp.float32).astype(jnp.bfloat16)
```

```python
import functools
import math

import jax
import jax.numpy as jnp
from jax import lax
from jax.experimental import pallas as pl
from jax.experimental.pallas import tpu as pltpu
from jax.sharding import PartitionSpec as P

HEAD_DIM = 128
ROWS = 128
LOCAL_HEADS = 4
X = 4
D = 2048
COLS = D // 2
NCOL = D // COLS
NEG = -1e30
MESH = pl.DeviceIdType.MESH
F32, BF16 = jnp.float32, jnp.bfloat16
SCALE = math.log2(math.e) / math.sqrt(HEAD_DIM)


def dot(a, b):
    return lax.dot_general(a, b, (((1,), (0,)), ((), ())), preferred_element_type=F32)


def dot_t(a, b):
    return lax.dot_general(a, b, (((1,), (1,)), ((), ())), preferred_element_type=F32)


def position(r, h):
    return jnp.where(
        r < 8,
        lax.rem(h, 16) + 16 * r,
        jnp.where(
            r < 16,
            lax.rem(h + 8, 16) + 16 * (r - 8),
            jnp.where(
                r < 32,
                lax.rem(h + 4, 8) + 8 * (r - 16),
                jnp.where(r < 64, lax.rem(h + 2, 4) + 4 * (r - 32), lax.rem(h + 1, 2) + 2 * (r - 64)),
            ),
        ),
    )


def kernel(
    q_ref, k_ref, v_ref, w_hbm, o_ref,
    perm, tiny, blocks, pre, r1, r2, r3, r4, l0, stat, top, den, num, ao, att, w_ref, part, out_buf, rs,
    s_w, s_tiny, s_p3, s_p2, s_p1, s_blk, s_fwd, s_chain, s_l0, s_ret, s_rs,
    r_blk, r_pre, r_1, r_2, r_3, r_4, r_l0, r_att, r_rs,
):
    s, x = lax.axis_index("seq"), lax.axis_index("head")
    c, i, g, y = lax.rem(s, 2), lax.rem(s // 2, 4), lax.rem(s // 8, 4), s // 32
    me = 2 * i + c
    base = s - me

    def group(y_, g_):
        return y_ * 32 + g_ * 8

    y_near = y + 1 - 2 * lax.rem(y, 2)
    g_near = g + 1 - 2 * lax.rem(g, 2)
    base_g1, base_g3 = group(y, g_near), group(y, 3 - g)
    base_y1, base_y3 = group(y_near, g), group(3 - y, g)
    upper1, upper2 = lax.rem(g, 2) == 1, g >= 2
    upper3, upper4 = lax.rem(y, 2) == 1, y >= 2
    lower1, lower2, lower3, lower4 = g - 2 * (g // 2) == 0, g < 2, lax.rem(y, 2) == 0, y < 2
    core0, core1 = c == 0, c == 1

    w_copy = pltpu.make_async_copy(w_hbm, w_ref, s_w)
    w_copy.start()

    barrier = pltpu.get_barrier_semaphore()

    def greet(s_, x_):
        pl.semaphore_signal(barrier, inc=1, device_id=(s_, x_), device_id_type=MESH)

    for n in range(8):
        for there in (base_g1, base_g3, base_y1, base_y3):
            if n % 2 == 1:
                greet(there + n, x)
            else:
                pl.when(core1)(functools.partial(greet, there + n, x))
        pl.when(me != n)(functools.partial(greet, base + n, x))
    for d in range(1, X):
        greet(s, lax.rem(x + d, X))

    row = lax.broadcasted_iota(jnp.int32, (ROWS, ROWS), 0)
    lane = lax.broadcasted_iota(jnp.int32, (ROWS, ROWS), 1)
    for j in range(LOCAL_HEADS):
        cols = slice(j * HEAD_DIM, (j + 1) * HEAD_DIM)
        pick = jnp.where(lane == position(row, LOCAL_HEADS * x + j), 1.0, 0.0).astype(BF16)
        picked = [dot(pick, ref[:, cols]) for ref in (q_ref, k_ref, v_ref)]
        for n in range(3):
            perm[j, n] = picked[n].astype(BF16)
        tiny[j] = jnp.concatenate([picked[1][:8], picked[2][:8]], axis=0).astype(BF16)

    pl.semaphore_wait(barrier, 26 + 16 * c)

    sends = []

    def send(cond, src, dst, ssem, rsem, s_, x_=None):
        copy = pltpu.make_async_remote_copy(
            src_ref=src, dst_ref=dst, send_sem=ssem, recv_sem=rsem,
            device_id=(s_, x if x_ is None else x_), device_id_type=MESH,
        )
        sends.append((cond, copy))
        if cond is None:
            copy.start()
        else:
            pl.when(cond)(copy.start)

    def arrived(ref, sem):
        pltpu.make_async_copy(ref, ref, sem).wait()

    for j in range(LOCAL_HEADS):
        send(lower4, tiny.at[j], r4.at[0, me], s_tiny.at[j], r_4.at[0], base_y3 + 2 * j + 1)
    for j in range(LOCAL_HEADS):
        send(lower3, perm.at[j, 1:3, 0:16], r3.at[0, me], s_p3.at[j], r_3.at[0], base_y1 + 2 * j + 1)
    for j in range(LOCAL_HEADS):
        send(lower2, perm.at[j, 1:3, 0:32], r2.at[0, me], s_p2.at[j], r_2.at[0], base_g3 + 2 * j + 1)
    for j in range(LOCAL_HEADS):
        send(me != 2 * j, perm.at[j], blocks.at[me], s_blk.at[j], r_blk.at[me], base + 2 * j)
    for j in range(LOCAL_HEADS):
        send(lower1, perm.at[j, 1:3, 0:64], r1.at[me], s_p1.at[j], r_1, base_g1 + 2 * j + 1)

    head = LOCAL_HEADS * x + i

    def send_back(b, lo):
        there = base + b
        pl.when(me != b)(
            pltpu.make_async_remote_copy(
                src_ref=ao.at[b], dst_ref=att.at[i, lo : lo + 64], send_sem=s_ret.at[b],
                recv_sem=r_att.at[i, lo // 64], device_id=(there, x), device_id_type=MESH,
            ).start
        )

        @pl.when(me == b)
        def _():
            att[i, lo : lo + 64] = ao[b]

    def wait_back(b, lo):
        pl.when(me != b)(
            pltpu.make_async_remote_copy(
                src_ref=ao.at[b], dst_ref=att.at[i, lo : lo + 64], send_sem=s_ret.at[b],
                recv_sem=r_att.at[i, lo // 64], device_id=(base + b, x), device_id_type=MESH,
            ).wait_send
        )

    @pl.when(core0)
    def _():
        blocks[me] = perm[i]

        def forward(b):
            return pltpu.make_async_remote_copy(
                src_ref=blocks.at[b, :, 0:64], dst_ref=pre.at[b], send_sem=s_fwd.at[b], recv_sem=r_pre.at[b],
                device_id=(s + 1, x), device_id_type=MESH,
            )

        def hand(b):
            return pltpu.make_async_remote_copy(
                src_ref=stat.at[b], dst_ref=l0.at[b], send_sem=s_l0.at[b], recv_sem=r_l0.at[b],
                device_id=(s + 1, x), device_id_type=MESH,
            )

        for b in range(8):
            pl.when(me != b)(functools.partial(arrived, blocks.at[b], r_blk.at[b]))
            forward(b).start()
        same = position(lane, head) <= position(row, head)
        half = lax.broadcasted_iota(jnp.int32, (64, ROWS), 1) < 64
        for b in range(8):
            width = ROWS * (b + 1)
            keys = blocks[0 : b + 1, 1].reshape(width, HEAD_DIM)
            values = blocks[0 : b + 1, 2].reshape(width, HEAD_DIM)
            scores = dot_t(blocks[b, 0], keys) * SCALE
            last = jnp.where(same, scores[:, ROWS * b :], NEG)
            scores = last if b == 0 else jnp.concatenate([scores[:, : ROWS * b], last], axis=1)
            peak = jnp.max(scores, axis=1, keepdims=True)
            weights = jnp.exp2(scores - peak)
            total = jnp.sum(weights, axis=1, keepdims=True)
            numer = dot(weights.astype(BF16), values)
            stat[b, 0] = numer[:64]
            stat[b, 1] = jnp.where(half, peak[:64], total[:64])
            hand(b).start()
            ao[b] = (numer[64:] / total[64:]).astype(BF16)
            send_back(b, 64)
        for b in range(8):
            forward(b).wait_send()
            hand(b).wait_send()
            wait_back(b, 64)

    @pl.when(core1)
    def _():
        twin1, twin3 = base_g1 + me, base_g3 + me
        twin_y1 = base_y1 + me

        def chain(n, src, dst, rsem, there):
            return pltpu.make_async_remote_copy(
                src_ref=src, dst_ref=dst, send_sem=s_chain.at[n], recv_sem=rsem,
                device_id=(there, x), device_id_type=MESH,
            )

        c4a = chain(0, r4.at[0], r4.at[1], r_4.at[1], twin_y1)
        c4b = chain(1, r4.at[0:2], r4.at[2:4], r_4.at[2], twin1)
        c4c = chain(2, r4.at[0:4], r4.at[4:8], r_4.at[3], twin3)
        c3a = chain(3, r3.at[0], r3.at[1], r_3.at[1], twin1)
        c3b = chain(4, r3.at[0:2], r3.at[2:4], r_3.at[2], twin3)
        c2a = chain(5, r2.at[0], r2.at[1], r_2.at[1], twin1)

        @pl.when(upper4)
        def _():
            arrived(r4.at[0], r_4.at[0])
            c4a.start()

        @pl.when(upper3)
        def _():
            arrived(r3.at[0], r_3.at[0])
            c3a.start()

        @pl.when(upper2)
        def _():
            arrived(r2.at[0], r_2.at[0])
            c2a.start()

        @pl.when(upper4)
        def _():
            arrived(r4.at[1], r_4.at[1])
            c4b.start()

        @pl.when(upper3)
        def _():
            arrived(r3.at[1], r_3.at[1])
            c3b.start()

        @pl.when(upper4)
        def _():
            arrived(r4.at[2:4], r_4.at[2])
            c4c.start()

        for b in range(8):
            arrived(pre.at[b], r_pre.at[b])

        def update(w, keys, values, mask=None, first=False, roll=False):
            nb = ROWS // w
            for b0 in range(0, 8, nb):
                at = (slice(b0, b0 + nb), slice(0, w))
                query = pre[b0 : b0 + nb, 0, 0:w].reshape(ROWS, HEAD_DIM)
                scores = dot_t(query, keys) * SCALE
                if mask is not None:
                    scores = jnp.where(mask(b0 * w, scores.shape), scores, NEG)
                peak = jnp.max(scores, axis=1, keepdims=True)
                if first:
                    peak = jnp.broadcast_to(peak, (ROWS, HEAD_DIM))
                else:
                    was = top[at].reshape(ROWS, HEAD_DIM)
                    peak = jnp.maximum(was, peak)
                    keep = jnp.exp2(was - peak)
                weights = jnp.exp2(scores - peak[:, :1])
                total = jnp.sum(weights, axis=1, keepdims=True)
                if roll:
                    weights = pltpu.roll(weights, 8, axis=1)
                numer = dot(weights.astype(BF16), values)
                if first:
                    total = jnp.broadcast_to(total, (ROWS, HEAD_DIM))
                else:
                    total = total + den[at].reshape(ROWS, HEAD_DIM) * keep
                    numer = numer + num[at].reshape(ROWS, HEAD_DIM) * keep
                top[at] = peak.reshape(nb, w, HEAD_DIM)
                den[at] = total.reshape(nb, w, HEAD_DIM)
                num[at] = numer.reshape(nb, w, HEAD_DIM)

        def place(n, w):
            return n // w * ROWS + position(lax.rem(n, w), head)

        def causal(w, start, shape):
            query = start + lax.broadcasted_iota(jnp.int32, shape, 0)
            key = lax.broadcasted_iota(jnp.int32, shape, 1)
            return place(key, w) <= place(query, w)

        def thin(start, shape):
            query = lax.broadcasted_iota(jnp.int32, shape, 0)
            key = lax.broadcasted_iota(jnp.int32, shape, 1)
            return (lax.rem(query, 16) < 8) & (lax.rem(key, 16) < 8)

        def thin_causal(start, shape):
            return thin(start, shape) & causal(16, start, shape)

        def own(n, w):
            return pre[:, n, 0:w].reshape(8 * w, HEAD_DIM)

        update(64, own(1, 64), own(2, 64), functools.partial(causal, 64), first=True)
        update(32, own(1, 32), own(2, 32), functools.partial(causal, 32))
        update(16, own(1, 16), own(2, 16), functools.partial(causal, 16))
        update(16, own(1, 16), own(2, 16), thin_causal)

        def level_rows(ref, n, w, rows):
            return ref[..., n, 0:w, :].reshape(rows, HEAD_DIM)

        @pl.when(upper2)
        def _():
            arrived(r2.at[1], r_2.at[1])
            update(32, level_rows(r2, 0, 32, 512), level_rows(r2, 1, 32, 512))
            keys, values = level_rows(r2, 0, 16, 256), level_rows(r2, 1, 16, 256)
            update(16, keys, values)
            update(16, keys, values, thin)

        @pl.when(upper3)
        def _():
            arrived(r3.at[2:4], r_3.at[2])
            keys, values = level_rows(r3, 0, 16, 512), level_rows(r3, 1, 16, 512)
            update(16, keys, values)
            update(16, keys, values, thin)

        @pl.when(upper4)
        def _():
            arrived(r4.at[4:8], r_4.at[3])
            both = r4[...].reshape(1024, HEAD_DIM)
            update(16, both, both, thin, roll=True)

        @pl.when(upper1)
        def _():
            arrived(r1, r_1)
            update(64, level_rows(r1, 0, 64, 512), level_rows(r1, 1, 64, 512))
            update(32, level_rows(r1, 0, 32, 256), level_rows(r1, 1, 32, 256))
            keys, values = level_rows(r1, 0, 16, 128), level_rows(r1, 1, 16, 128)
            update(16, keys, values)
            update(16, keys, values, thin)

        for b in range(8):
            arrived(l0.at[b], r_l0.at[b])
            peak, total = l0[b, 1, :, 0:1], l0[b, 1, :, 64:65]
            was = top[b]
            best = jnp.maximum(was, peak)
            keep, gain = jnp.exp2(was - best), jnp.exp2(peak - best)
            numer = num[b] * keep + l0[b, 0] * gain
            total = den[b] * keep + total * gain
            ao[b] = (numer / total).astype(BF16)
            send_back(b, 0)
        for b in range(8):
            wait_back(b, 0)

        @pl.when(upper4)
        def _():
            c4a.wait_send()
            c4b.wait_send()
            c4c.wait_send()

        @pl.when(upper3)
        def _():
            c3a.wait_send()
            c3b.wait_send()

        @pl.when(upper2)
        def _():
            c2a.wait_send()

    w_copy.wait()
    heads = []
    for j in range(LOCAL_HEADS):
        for half in range(2):
            sender = 2 * j + (1 - half)
            pl.when(me != sender)(
                functools.partial(arrived, att.at[j, 64 * half : 64 * half + 64], r_att.at[j, half])
            )
        pick = jnp.where(row == position(lane, LOCAL_HEADS * x + j), 1.0, 0.0).astype(BF16)
        heads.append(dot(pick, att[j]).astype(BF16))
    attention = jnp.concatenate(heads, axis=1)
    for n in range(NCOL):
        cols = slice(n * COLS, (n + 1) * COLS)
        product = dot(attention, w_ref[:, cols])
        part[n] = product
        out_buf[n] = product.astype(BF16)
        for d in range(1, X):
            there = lax.rem(x + d, X)
            send(
                None, out_buf.at[n, pl.ds(pl.multiple_of(32 * there, 32), 32)], rs.at[n, d - 1],
                s_rs.at[n, d - 1], r_rs.at[n, d - 1], s, there,
            )
    for n in range(NCOL):
        total = part[n, pl.ds(pl.multiple_of(32 * x, 32), 32)]
        for d in range(1, X):
            arrived(rs.at[n, d - 1], r_rs.at[n, d - 1])
            total = total + rs[n, d - 1].astype(F32)
        o_ref[:, n * COLS : (n + 1) * COLS] = total.astype(BF16)
    for cond, copy in sends:
        if cond is None:
            copy.wait_send()
        else:
            pl.when(cond)(copy.wait_send)


def per_device(query_rows, key_rows, value_rows, out_weight):
    vmem = pl.BlockSpec(memory_space=pltpu.VMEM)
    dma = pltpu.SemaphoreType.DMA
    hd = HEAD_DIM
    return pl.pallas_call(
        kernel,
        out_shape=jax.ShapeDtypeStruct((ROWS // X, D), BF16),
        in_specs=[vmem, vmem, vmem, pl.BlockSpec(memory_space=pl.ANY)],
        out_specs=vmem,
        scratch_shapes=[
            pltpu.VMEM((LOCAL_HEADS, 3, ROWS, hd), BF16),
            pltpu.VMEM((LOCAL_HEADS, 16, hd), BF16),
            pltpu.VMEM((8, 3, ROWS, hd), BF16),
            pltpu.VMEM((8, 3, 64, hd), BF16),
            pltpu.VMEM((8, 2, 64, hd), BF16),
            pltpu.VMEM((2, 8, 2, 32, hd), BF16),
            pltpu.VMEM((4, 8, 2, 16, hd), BF16),
            pltpu.VMEM((8, 8, 16, hd), BF16),
            pltpu.VMEM((8, 2, 64, hd), F32),
            pltpu.VMEM((8, 2, 64, hd), F32),
            pltpu.VMEM((8, 64, hd), F32),
            pltpu.VMEM((8, 64, hd), F32),
            pltpu.VMEM((8, 64, hd), F32),
            pltpu.VMEM((8, 64, hd), BF16),
            pltpu.VMEM((LOCAL_HEADS, ROWS, hd), BF16),
            pltpu.VMEM((LOCAL_HEADS * hd, D), BF16),
            pltpu.VMEM((NCOL, ROWS, COLS), F32),
            pltpu.VMEM((NCOL, ROWS, COLS), BF16),
            pltpu.VMEM((NCOL, X - 1, ROWS // X, COLS), BF16),
            dma, dma((4,)), dma((4,)), dma((4,)), dma((4,)), dma((4,)), dma((8,)), dma((6,)),
            dma((8,)), dma((8,)), dma((NCOL, X - 1)),
            dma((8,)), dma((8,)), dma, dma((2,)), dma((3,)), dma((4,)), dma((8,)), dma((4, 2)),
            dma((NCOL, X - 1)),
        ],
        compiler_params=pltpu.CompilerParams(
            collective_id=0, has_side_effects=True, vmem_limit_bytes=48 * 1024 * 1024
        ),
    )(query_rows, key_rows, value_rows, out_weight)


def solution(mesh):
    in_specs = (P("seq", "head"), P("seq", "head"), P("seq", "head"), P("head", None))
    return jax.shard_map(
        per_device, mesh=mesh, in_specs=in_specs, out_specs=P(("seq", "head"), None), check_vma=False
    )
```

```python
import functools
import math

import jax
import jax.numpy as jnp
from jax import lax
from jax.experimental import pallas as pl
from jax.experimental.pallas import tpu as pltpu
from jax.sharding import PartitionSpec as P

HEAD_DIM = 128
ROWS = 128
LOCAL_HEADS = 4
X = 4
D = 2048
COLS = D // 2
NCOL = D // COLS
NEG = -1e30
MESH = pl.DeviceIdType.MESH
F32, BF16 = jnp.float32, jnp.bfloat16
SCALE = math.log2(math.e) / math.sqrt(HEAD_DIM)


def dot(a, b):
    return lax.dot_general(a, b, (((1,), (0,)), ((), ())), preferred_element_type=F32)


def dot_t(a, b):
    return lax.dot_general(a, b, (((1,), (1,)), ((), ())), preferred_element_type=F32)


def position(r, h):
    return jnp.where(
        r < 8,
        lax.rem(h, 16) + 16 * r,
        jnp.where(
            r < 16,
            lax.rem(h + 8, 16) + 16 * (r - 8),
            jnp.where(
                r < 32,
                lax.rem(h + 4, 8) + 8 * (r - 16),
                jnp.where(r < 64, lax.rem(h + 2, 4) + 4 * (r - 32), lax.rem(h + 1, 2) + 2 * (r - 64)),
            ),
        ),
    )


def kernel(
    q_hbm, k_hbm, v_hbm, w_hbm, o_ref,
    q_ref, k_ref, v_ref, perm, blocks, pre, r1, r2, rv, ry, l0, stat, top, den, num, ao, att, w_ref, part, out_buf, rs,
    go, s_in, s_w, s_p1, s_p2, s_pv, s_blk, s_fwd, s_y, s_l0, s_ret, s_rs,
    r_blk, r_pre, r_1, r_2, r_v, r_y, r_l0, r_att, r_rs,
):
    s, x = lax.axis_index("seq"), lax.axis_index("head")
    c, i, g, y = lax.rem(s, 2), lax.rem(s // 2, 4), lax.rem(s // 8, 4), s // 32
    me = 2 * i + c
    base = s - me

    line = y * 32
    upper1, upper2 = lax.rem(g, 2) == 1, g >= 2
    lower1, lower2 = lax.rem(g, 2) == 0, g < 2
    core0, core1 = c == 0, c == 1

    loads = [
        pltpu.make_async_copy(src, dst, s_in.at[n])
        for n, (src, dst) in enumerate(((q_hbm, q_ref), (k_hbm, k_ref), (v_hbm, v_ref)))
    ]
    for load in loads:
        load.start()
    w_copy = pltpu.make_async_copy(w_hbm, w_ref, s_w)
    w_copy.start()

    barrier = pltpu.get_barrier_semaphore()

    def greet(s_, x_):
        pl.semaphore_signal(barrier, inc=1, device_id=(s_, x_), device_id_type=MESH)

    @pl.when(core0)
    def _():
        for n in range(0, 8, 2):
            pl.when(me != n)(functools.partial(greet, base + n, x))

    @pl.when(core1)
    def _():
        for n in range(0, 8, 2):
            greet(base + n, x)
        for d in range(1, 4):
            for n in range(1, 8, 2):
                greet(line + 8 * lax.rem(g + d, 4) + n, x)
            greet(lax.rem(s + 32 * d, 128), x)

    for d in range(1, X):
        greet(s, lax.rem(x + d, X))

    for load in loads:
        load.wait()
    row = lax.broadcasted_iota(jnp.int32, (ROWS, ROWS), 0)
    lane = lax.broadcasted_iota(jnp.int32, (ROWS, ROWS), 1)
    for j in range(LOCAL_HEADS):
        cols = slice(j * HEAD_DIM, (j + 1) * HEAD_DIM)
        pick = jnp.where(lane == position(row, LOCAL_HEADS * x + j), 1.0, 0.0).astype(BF16)
        for n, ref in enumerate((q_ref, k_ref, v_ref)):
            perm[j, n] = dot(pick, ref[:, cols]).astype(BF16)

    @pl.when(core0)
    def _():
        pl.semaphore_wait(barrier, 10)
        for n in range(1, 8, 2):
            pl.semaphore_signal(go, inc=1, device_id=(base + n, x), device_id_type=MESH)

    @pl.when(core1)
    def _():
        pl.semaphore_wait(go, 4)


    sends = []

    def send(cond, src, dst, ssem, rsem, s_, x_=None):
        copy = pltpu.make_async_remote_copy(
            src_ref=src, dst_ref=dst, send_sem=ssem, recv_sem=rsem,
            device_id=(s_, x if x_ is None else x_), device_id_type=MESH,
        )
        sends.append((cond, copy))
        if cond is None:
            copy.start()
        else:
            pl.when(cond)(copy.start)

    def arrived(ref, sem):
        pltpu.make_async_copy(ref, ref, sem).wait()

    def regroup(cond):
        for j in range(LOCAL_HEADS):
            send(
                cond & (me != 2 * j), perm.at[j], blocks.at[me], s_blk.at[j], r_blk.at[me], base + 2 * j
            )

    regroup(g < 2)

    @pl.when(core1)
    def _():
        pl.semaphore_wait(barrier, 18)
        pl.semaphore_signal(go, inc=1, device_id=(s - 1, x), device_id_type=MESH)

    @pl.when(core0)
    def _():
        pl.semaphore_wait(go, 1)

    for h in range(4):
        for j in range(LOCAL_HEADS):
            cond = (y < 3) & (g >= h) & ((g != h) | (me != 2 * j + 1))
            send(cond, perm.at[j, 1:3, 0:16], rv.at[g, me], s_pv.at[h, j], r_v.at[g], line + 8 * h + 2 * j + 1)

    @pl.when((y < 3) & core1)
    def _():
        rv[g, me] = perm[i, 1:3, 0:16]

    for h in range(2):
        for j in range(LOCAL_HEADS):
            send(
                lower2, perm.at[j, 1:3, 0:32], r2.at[g, me], s_p2.at[h, j], r_2.at[g],
                line + 8 * (2 + h) + 2 * j + 1,
            )
    for j in range(LOCAL_HEADS):
        send(lower1, perm.at[j, 1:3, 0:64], r1.at[me], s_p1.at[j], r_1, base + 8 + 2 * j + 1)
    regroup(g >= 2)

    head = LOCAL_HEADS * x + i

    def send_back(b, lo):
        there = base + b
        pl.when(me != b)(
            pltpu.make_async_remote_copy(
                src_ref=ao.at[b], dst_ref=att.at[i, lo : lo + 64], send_sem=s_ret.at[b],
                recv_sem=r_att.at[i, lo // 64], device_id=(there, x), device_id_type=MESH,
            ).start
        )

        @pl.when(me == b)
        def _():
            att[i, lo : lo + 64] = ao[b]

    def wait_back(b, lo):
        pl.when(me != b)(
            pltpu.make_async_remote_copy(
                src_ref=ao.at[b], dst_ref=att.at[i, lo : lo + 64], send_sem=s_ret.at[b],
                recv_sem=r_att.at[i, lo // 64], device_id=(base + b, x), device_id_type=MESH,
            ).wait_send
        )

    @pl.when(core0)
    def _():
        blocks[me] = perm[i]

        def forward(b):
            return pltpu.make_async_remote_copy(
                src_ref=blocks.at[b, :, 0:64], dst_ref=pre.at[b], send_sem=s_fwd.at[b], recv_sem=r_pre.at[b],
                device_id=(s + 1, x), device_id_type=MESH,
            )

        def hand(b):
            return pltpu.make_async_remote_copy(
                src_ref=stat.at[b], dst_ref=l0.at[b], send_sem=s_l0.at[b], recv_sem=r_l0.at[b],
                device_id=(s + 1, x), device_id_type=MESH,
            )

        for b in range(8):
            pl.when(me != b)(functools.partial(arrived, blocks.at[b], r_blk.at[b]))
            forward(b).start()
        same = position(lane, head) <= position(row, head)
        half = lax.broadcasted_iota(jnp.int32, (64, ROWS), 1) < 64
        for b in range(8):
            width = ROWS * (b + 1)
            keys = blocks[0 : b + 1, 1].reshape(width, HEAD_DIM)
            values = blocks[0 : b + 1, 2].reshape(width, HEAD_DIM)
            scores = dot_t(blocks[b, 0], keys) * SCALE
            last = jnp.where(same, scores[:, ROWS * b :], NEG)
            scores = last if b == 0 else jnp.concatenate([scores[:, : ROWS * b], last], axis=1)
            peak = jnp.max(scores, axis=1, keepdims=True)
            weights = jnp.exp2(scores - peak)
            total = jnp.sum(weights, axis=1, keepdims=True)
            numer = dot(weights.astype(BF16), values)
            stat[b, 0] = numer[:64]
            stat[b, 1] = jnp.where(half, peak[:64], total[:64])
            hand(b).start()
            ao[b] = (numer[64:] / total[64:]).astype(BF16)
            send_back(b, 64)
        for b in range(8):
            forward(b).wait_send()
            hand(b).wait_send()
            wait_back(b, 64)

    @pl.when(core1)
    def _():
        def arrived_if(cond, ref, sem):
            pl.when(cond)(functools.partial(arrived, ref, sem))

        passes = []

        def pass_on(cond, h, src):
            for d in range(1, 4):
                copy = pltpu.make_async_remote_copy(
                    src_ref=src, dst_ref=ry.at[y, h], send_sem=s_y.at[d - 1, h], recv_sem=r_y.at[y],
                    device_id=(s + 32 * d, x), device_id_type=MESH,
                )
                pl.when(cond & (y + d < 4))(copy.start)
                passes.append((cond & (y + d < 4), copy))

        for h in range(4):
            later = (y < 3) & (g <= h)
            arrived_if(later & (g != h), rv.at[h], r_v.at[h])
            arrived_if(later & (g == h), rv.at[h, 0:7], r_v.at[h])
            pass_on(later, h, rv.at[h])
        for h in range(2):
            arrived_if(upper2, r2.at[h], r_2.at[h])
            pass_on(upper2, h, r2.at[h, :, :, 0:16])
        arrived_if(upper1, r1, r_1)
        for h in (0, 2):
            pass_on(g == h + 1, h, r1.at[:, :, 0:16])

        for b in range(8):
            arrived(pre.at[b], r_pre.at[b])

        def update(w, keys, values, mask=None, first=False):
            nb = ROWS // w
            for b0 in range(0, 8, nb):
                at = (slice(b0, b0 + nb), slice(0, w))
                query = pre[b0 : b0 + nb, 0, 0:w].reshape(ROWS, HEAD_DIM)
                scores = dot_t(query, keys) * SCALE
                if mask is not None:
                    scores = jnp.where(mask(b0 * w, scores.shape), scores, NEG)
                peak = jnp.max(scores, axis=1, keepdims=True)
                if first:
                    peak = jnp.broadcast_to(peak, (ROWS, HEAD_DIM))
                else:
                    was = top[at].reshape(ROWS, HEAD_DIM)
                    peak = jnp.maximum(was, peak)
                    keep = jnp.exp2(was - peak)
                weights = jnp.exp2(scores - peak[:, :1])
                total = jnp.sum(weights, axis=1, keepdims=True)
                numer = dot(weights.astype(BF16), values)
                if first:
                    total = jnp.broadcast_to(total, (ROWS, HEAD_DIM))
                else:
                    total = total + den[at].reshape(ROWS, HEAD_DIM) * keep
                    numer = numer + num[at].reshape(ROWS, HEAD_DIM) * keep
                top[at] = peak.reshape(nb, w, HEAD_DIM)
                den[at] = total.reshape(nb, w, HEAD_DIM)
                num[at] = numer.reshape(nb, w, HEAD_DIM)

        def place(n, w):
            return n // w * ROWS + position(lax.rem(n, w), head)

        def causal(w, start, shape):
            query = start + lax.broadcasted_iota(jnp.int32, shape, 0)
            key = lax.broadcasted_iota(jnp.int32, shape, 1)
            return place(key, w) <= place(query, w)

        def thin(start, shape):
            query = lax.broadcasted_iota(jnp.int32, shape, 0)
            key = lax.broadcasted_iota(jnp.int32, shape, 1)
            return (lax.rem(query, 16) < 8) & (lax.rem(key, 16) < 8)

        def thin_causal(start, shape):
            return thin(start, shape) & causal(16, start, shape)

        def own(n, w):
            return pre[:, n, 0:w].reshape(8 * w, HEAD_DIM)

        update(64, own(1, 64), own(2, 64), functools.partial(causal, 64), first=True)
        update(32, own(1, 32), own(2, 32), functools.partial(causal, 32))
        update(16, own(1, 16), own(2, 16), functools.partial(causal, 16))
        update(16, own(1, 16), own(2, 16), thin_causal)

        def level_rows(ref, n, w, rows):
            return ref[..., n, 0:w, :].reshape(rows, HEAD_DIM)

        @pl.when(upper1)
        def _():
            update(64, level_rows(r1, 0, 64, 512), level_rows(r1, 1, 64, 512))
            update(32, level_rows(r1, 0, 32, 256), level_rows(r1, 1, 32, 256))
            keys, values = level_rows(r1, 0, 16, 128), level_rows(r1, 1, 16, 128)
            update(16, keys, values)
            update(16, keys, values, thin)

        @pl.when(upper2)
        def _():
            update(32, level_rows(r2, 0, 32, 512), level_rows(r2, 1, 32, 512))
            keys, values = level_rows(r2, 0, 16, 256), level_rows(r2, 1, 16, 256)
            update(16, keys, values)
            update(16, keys, values, thin)

        for t in range(3):

            @pl.when(y > t)
            def _(t=t):
                arrived(ry.at[t], r_y.at[t])
                keys = ry[t, :, :, 0].reshape(512, HEAD_DIM)
                values = ry[t, :, :, 1].reshape(512, HEAD_DIM)
                if t % 2 == 0:
                    pl.when(y == t + 1)(functools.partial(update, 16, keys, values))
                update(16, keys, values, thin)

        for b in range(8):
            arrived(l0.at[b], r_l0.at[b])
            peak, total = l0[b, 1, :, 0:1], l0[b, 1, :, 64:65]
            was = top[b]
            best = jnp.maximum(was, peak)
            keep, gain = jnp.exp2(was - best), jnp.exp2(peak - best)
            numer = num[b] * keep + l0[b, 0] * gain
            total = den[b] * keep + total * gain
            ao[b] = (numer / total).astype(BF16)
            send_back(b, 0)
        for b in range(8):
            wait_back(b, 0)

        for cond, copy in passes:
            pl.when(cond)(copy.wait_send)

    w_copy.wait()
    heads = []
    for j in range(LOCAL_HEADS):
        for half in range(2):
            sender = 2 * j + (1 - half)
            pl.when(me != sender)(
                functools.partial(arrived, att.at[j, 64 * half : 64 * half + 64], r_att.at[j, half])
            )
        pick = jnp.where(row == position(lane, LOCAL_HEADS * x + j), 1.0, 0.0).astype(BF16)
        heads.append(dot(pick, att[j]).astype(BF16))
    attention = jnp.concatenate(heads, axis=1)
    for n in range(NCOL):
        cols = slice(n * COLS, (n + 1) * COLS)
        product = dot(attention, w_ref[:, cols])
        part[n] = product
        out_buf[n] = product.astype(BF16)
        for d in range(1, X):
            there = lax.rem(x + d, X)
            send(
                None, out_buf.at[n, pl.ds(pl.multiple_of(32 * there, 32), 32)], rs.at[n, d - 1],
                s_rs.at[n, d - 1], r_rs.at[n, d - 1], s, there,
            )
    for n in range(NCOL):
        total = part[n, pl.ds(pl.multiple_of(32 * x, 32), 32)]
        for d in range(1, X):
            arrived(rs.at[n, d - 1], r_rs.at[n, d - 1])
            total = total + rs[n, d - 1].astype(F32)
        o_ref[:, n * COLS : (n + 1) * COLS] = total.astype(BF16)
    for cond, copy in sends:
        if cond is None:
            copy.wait_send()
        else:
            pl.when(cond)(copy.wait_send)


def per_device(query_rows, key_rows, value_rows, out_weight):
    vmem = pl.BlockSpec(memory_space=pltpu.VMEM)
    dma = pltpu.SemaphoreType.DMA
    hd = HEAD_DIM
    return pl.pallas_call(
        kernel,
        out_shape=jax.ShapeDtypeStruct((ROWS // X, D), BF16),
        in_specs=[pl.BlockSpec(memory_space=pl.ANY)] * 4,
        out_specs=vmem,
        scratch_shapes=[
            pltpu.VMEM((ROWS, LOCAL_HEADS * hd), BF16),
            pltpu.VMEM((ROWS, LOCAL_HEADS * hd), BF16),
            pltpu.VMEM((ROWS, LOCAL_HEADS * hd), BF16),
            pltpu.VMEM((LOCAL_HEADS, 3, ROWS, hd), BF16),
            pltpu.VMEM((8, 3, ROWS, hd), BF16),
            pltpu.VMEM((8, 3, 64, hd), BF16),
            pltpu.VMEM((8, 2, 64, hd), BF16),
            pltpu.VMEM((2, 8, 2, 32, hd), BF16),
            pltpu.VMEM((4, 8, 2, 16, hd), BF16),
            pltpu.VMEM((3, 4, 8, 2, 16, hd), BF16),
            pltpu.VMEM((8, 2, 64, hd), F32),
            pltpu.VMEM((8, 2, 64, hd), F32),
            pltpu.VMEM((8, 64, hd), F32),
            pltpu.VMEM((8, 64, hd), F32),
            pltpu.VMEM((8, 64, hd), F32),
            pltpu.VMEM((8, 64, hd), BF16),
            pltpu.VMEM((LOCAL_HEADS, ROWS, hd), BF16),
            pltpu.VMEM((LOCAL_HEADS * hd, D), BF16),
            pltpu.VMEM((NCOL, ROWS, COLS), F32),
            pltpu.VMEM((NCOL, ROWS, COLS), BF16),
            pltpu.VMEM((NCOL, X - 1, ROWS // X, COLS), BF16),
            pltpu.SemaphoreType.REGULAR,
            dma((3,)), dma, dma((4,)), dma((2, 4)), dma((4, 4)), dma((4,)), dma((8,)), dma((3, 4)),
            dma((8,)), dma((8,)), dma((NCOL, X - 1)),
            dma((8,)), dma((8,)), dma, dma((2,)), dma((4,)), dma((3,)), dma((8,)), dma((4, 2)),
            dma((NCOL, X - 1)),
        ],
        compiler_params=pltpu.CompilerParams(
            collective_id=0, has_side_effects=True, vmem_limit_bytes=60 * 1024 * 1024
        ),
    )(query_rows, key_rows, value_rows, out_weight)


def solution(mesh):
    in_specs = (P("seq", "head"), P("seq", "head"), P("seq", "head"), P("head", None))
    return jax.shard_map(
        per_device, mesh=mesh, in_specs=in_specs, out_specs=P(("seq", "head"), None), check_vma=False
    )
```

```python
import functools
import math

import jax
import jax.numpy as jnp
from jax import lax
from jax.experimental import pallas as pl
from jax.experimental.pallas import tpu as pltpu
from jax.sharding import PartitionSpec as P

HEAD_DIM = 128
ROWS = 128
LOCAL_HEADS = 4
X = 4
D = 2048
COLS = D // 4
CHUNK = 128
NEG = -1e30
MESH = pl.DeviceIdType.MESH
F32, BF16 = jnp.float32, jnp.bfloat16
SCALE = math.log2(math.e) / math.sqrt(HEAD_DIM)

def dot(a, b):
    return lax.dot_general(a, b, (((1,), (0,)), ((), ())), preferred_element_type=F32)

def dot_t(a, b):
    return lax.dot_general(a, b, (((1,), (1,)), ((), ())), preferred_element_type=F32)

def position(r, h):
    return jnp.where(
        r < 8,
        lax.rem(h, 16) + 16 * r,
        jnp.where(
            r < 16,
            lax.rem(h + 8, 16) + 16 * (r - 8),
            jnp.where(
                r < 32,
                lax.rem(h + 4, 8) + 8 * (r - 16),
                jnp.where(r < 64, lax.rem(h + 2, 4) + 4 * (r - 32), lax.rem(h + 1, 2) + 2 * (r - 64)),
            ),
        ),
    )

def kernel(
    q_hbm, k_hbm, v_hbm, w_hbm, o_ref,
    q_ref, k_ref, v_ref, perm, blocks, pre, r1, r2, rv, ry, rp, pack, l0, stat, top, den, num, ao, att, nat, ax, w_ref, part,
    go, s_in, s_w, s_p1, s_p2, s_pv, s_blk, s_fwd, s_y, s_l0, s_ret, s_ax, s_wx, s_wf, s_wy, s_ws,
    r_blk, r_pre, r_1, r_2, r_v, r_y, r_l0, r_att, r_ax, r_wx, r_wf, r_wy, r_ws,
):
    s, x = lax.axis_index("seq"), lax.axis_index("head")
    c, i, g, y = lax.rem(s, 2), lax.rem(s // 2, 4), lax.rem(s // 8, 4), s // 32
    me = 2 * i + c
    base = s - me

    line = y * 32
    s_up, s_down = lax.rem(s + 32, 128), lax.rem(s + 96, 128)
    upper1, upper2 = lax.rem(g, 2) == 1, g >= 2
    lower1, lower2 = lax.rem(g, 2) == 0, g < 2
    core0, core1 = c == 0, c == 1

    loads = [
        pltpu.make_async_copy(src, dst, s_in.at[n])
        for n, (src, dst) in enumerate(((q_hbm, q_ref), (k_hbm, k_ref), (v_hbm, v_ref)))
    ]
    for load in loads:
        load.start()
    w_copy = pltpu.make_async_copy(w_hbm, w_ref.at[x], s_w)
    w_copy.start()

    barrier = pltpu.get_barrier_semaphore()

    def greet(s_, x_):
        pl.semaphore_signal(barrier, inc=1, device_id=(s_, x_), device_id_type=MESH)

    @pl.when(core0)
    def _():
        for n in range(0, 8, 2):
            pl.when(me != n)(functools.partial(greet, base + n, x))
        greet(s_up, x)
        greet(s_down, x)

    @pl.when(core1)
    def _():
        for n in range(0, 8, 2):
            greet(base + n, x)
        for d in range(1, 4):
            for n in range(1, 8, 2):
                greet(line + 8 * lax.rem(g + d, 4) + n, x)
            greet(lax.rem(s + 32 * d, 128), x)

    for d in range(1, X):
        greet(s, lax.rem(x + d, X))

    for load in loads:
        load.wait()
    row = lax.broadcasted_iota(jnp.int32, (ROWS, ROWS), 0)
    lane = lax.broadcasted_iota(jnp.int32, (ROWS, ROWS), 1)
    for j in range(LOCAL_HEADS):
        cols = slice(j * HEAD_DIM, (j + 1) * HEAD_DIM)
        pick = jnp.where(lane == position(row, LOCAL_HEADS * x + j), 1.0, 0.0).astype(BF16)
        for n, ref in enumerate((q_ref, k_ref, v_ref)):
            perm[j, n] = dot(pick, ref[:, cols]).astype(BF16)

    @pl.when(core0)
    def _():
        pl.semaphore_wait(barrier, 12)
        for n in range(1, 8, 2):
            pl.semaphore_signal(go, inc=1, device_id=(base + n, x), device_id_type=MESH)

    @pl.when(core1)
    def _():
        pl.semaphore_wait(go, 4)

    sends = []

    def send(cond, src, dst, ssem, rsem, s_, x_=None):
        copy = pltpu.make_async_remote_copy(
            src_ref=src, dst_ref=dst, send_sem=ssem, recv_sem=rsem,
            device_id=(s_, x if x_ is None else x_), device_id_type=MESH,
        )
        sends.append((cond, copy))
        if cond is None:
            copy.start()
        else:
            pl.when(cond)(copy.start)

    def arrived(ref, sem):
        pltpu.make_async_copy(ref, ref, sem).wait()

    def regroup(cond):
        for n in range(2):
            part_rows = slice(64 * n, 64 * n + 64)
            for j in range(LOCAL_HEADS):
                send(
                    cond & (me != 2 * j), perm.at[j, :, part_rows], blocks.at[me, :, part_rows],
                    s_blk.at[n, j], r_blk.at[n, me], base + 2 * j,
                )

    regroup(g < 2)

    x_left, x_right, x_far = lax.rem(x + 3, X), lax.rem(x + 1, X), lax.rem(x + 2, X)
    around = (x_left, x_right, x_far)
    mine = 2 * lax.rem(y, 2)
    theirs = 2 - mine
    w_copy.wait()

    def weight(x_, k):
        return w_ref.at[x_, pl.ds(pl.multiple_of(k * CHUNK, CHUNK), CHUNK)]

    def weight_copy(x_, k, s_, to, ssem, rsem):
        return pltpu.make_async_remote_copy(
            src_ref=weight(x_, k), dst_ref=weight(x_, k), send_sem=ssem, recv_sem=rsem,
            device_id=(s_, to), device_id_type=MESH,
        )

    def own_copy(m, side):
        to = (x_right, x_left)[side]
        return weight_copy(x, mine + m, s, to, s_wx.at[side, m], r_wx.at[side, m])

    def far_copy(m):
        to = (x_right, x_left)[m]
        return weight_copy(around[m], mine + m, s, to, s_wf.at[m], r_wf.at[m])

    def line_copy(n, m):
        to = (s_up, s_down)[m]
        return weight_copy(around[n], mine + m, to, x, s_wy.at[n, m], r_wy.at[n, m])

    def share_mine(n, m):
        return weight_copy(around[n], mine + m, s + 1, x, s_ws.at[n, m], r_ws.at[n])

    def share_theirs(n, m):
        return weight_copy(around[n], theirs + m, s + 1, x, s_ws.at[n, 2 + m], r_ws.at[n])

    def take_theirs(n):
        for m in range(2):
            arrived(weight(around[n], theirs + m), r_wy.at[n, m])
            share_theirs(n, m).start()

    @pl.when(core0)
    def _():
        for m in range(2):
            own_copy(m, 0).start()
            own_copy(1 - m, 1).start()

    @pl.when(core1)
    def _():
        pl.semaphore_wait(barrier, 18)
        pl.semaphore_signal(go, inc=1, device_id=(s - 1, x), device_id_type=MESH)

    @pl.when(core0)
    def _():
        pl.semaphore_wait(go, 1)

    for h in range(4):
        for j in range(LOCAL_HEADS):
            cond = (y < 3) & (g >= h) & ((g != h) | (me != 2 * j + 1))
            send(cond, perm.at[j, 1:3, 0:16], rv.at[g, me], s_pv.at[h, j], r_v.at[g], line + 8 * h + 2 * j + 1)

    @pl.when((y < 3) & core1)
    def _():
        rv[g, me] = perm[i, 1:3, 0:16]

    for h in range(2):
        for j in range(LOCAL_HEADS):
            send(
                lower2, perm.at[j, 1:3, 0:32], r2.at[g, me], s_p2.at[h, j], r_2.at[g],
                line + 8 * (2 + h) + 2 * j + 1,
            )
    for j in range(LOCAL_HEADS):
        send(lower1, perm.at[j, 1:3, 0:64], r1.at[me], s_p1.at[j], r_1, base + 8 + 2 * j + 1)
    regroup(g >= 2)

    head = LOCAL_HEADS * x + i

    def send_back(b, lo):
        there = base + b
        pl.when(me != b)(
            pltpu.make_async_remote_copy(
                src_ref=ao.at[b], dst_ref=att.at[i, lo : lo + 64], send_sem=s_ret.at[b],
                recv_sem=r_att.at[i, lo // 64], device_id=(there, x), device_id_type=MESH,
            ).start
        )

        @pl.when(me == b)
        def _():
            att[i, lo : lo + 64] = ao[b]

    def wait_back(b, lo):
        pl.when(me != b)(
            pltpu.make_async_remote_copy(
                src_ref=ao.at[b], dst_ref=att.at[i, lo : lo + 64], send_sem=s_ret.at[b],
                recv_sem=r_att.at[i, lo // 64], device_id=(base + b, x), device_id_type=MESH,
            ).wait_send
        )

    @pl.when(core0)
    def _():
        blocks[me] = perm[i]

        def forward(b):
            return pltpu.make_async_remote_copy(
                src_ref=blocks.at[b, :, 0:64], dst_ref=pre.at[b], send_sem=s_fwd.at[b], recv_sem=r_pre.at[b],
                device_id=(s + 1, x), device_id_type=MESH,
            )

        def hand(b):
            return pltpu.make_async_remote_copy(
                src_ref=stat.at[b], dst_ref=l0.at[b], send_sem=s_l0.at[b], recv_sem=r_l0.at[b],
                device_id=(s + 1, x), device_id_type=MESH,
            )

        for side in range(2):
            m = side
            arrived(weight(around[side], mine + m), r_wx.at[side, m])
            far_copy(m).start()
            line_copy(side, m).start()
            share_mine(side, m).start()

        for b in range(8):
            pl.when(me != b)(functools.partial(arrived, blocks.at[b, :, 0:64], r_blk.at[0, b]))
            forward(b).start()
        for side in range(2):
            m = 1 - side
            arrived(weight(around[side], mine + m), r_wx.at[side, m])
            line_copy(side, m).start()
            share_mine(side, m).start()

        for b in range(8):
            pl.when(me != b)(functools.partial(arrived, blocks.at[b, :, 64:128], r_blk.at[1, b]))
        same = position(lane, head) <= position(row, head)
        half = lax.broadcasted_iota(jnp.int32, (64, ROWS), 1) < 64
        for b in range(8):
            width = ROWS * (b + 1)
            keys = blocks[0 : b + 1, 1].reshape(width, HEAD_DIM)
            values = blocks[0 : b + 1, 2].reshape(width, HEAD_DIM)
            scores = dot_t(blocks[b, 0], keys) * SCALE
            last = jnp.where(same, scores[:, ROWS * b :], NEG)
            scores = last if b == 0 else jnp.concatenate([scores[:, : ROWS * b], last], axis=1)
            peak = jnp.max(scores, axis=1, keepdims=True)
            weights = jnp.exp2(scores - peak)
            total = jnp.sum(weights, axis=1, keepdims=True)
            numer = dot(weights.astype(BF16), values)
            stat[b, 0] = numer[:64]
            stat[b, 1] = jnp.where(half, peak[:64], total[:64])
            hand(b).start()
            ao[b] = (numer[64:] / total[64:]).astype(BF16)
            send_back(b, 64)
        for m in range(2):
            arrived(weight(x_far, mine + m), r_wf.at[m])
            line_copy(2, m).start()
            share_mine(2, m).start()
        take_theirs(0)
        take_theirs(1)

        for b in range(8):
            forward(b).wait_send()
            hand(b).wait_send()
            wait_back(b, 64)

    @pl.when(core1)
    def _():
        def arrived_if(cond, ref, sem):
            pl.when(cond)(functools.partial(arrived, ref, sem))

        passes = []

        def pass_on(cond, h, src):
            def to_line(where, d, src, dst, rsem):
                copy = pltpu.make_async_remote_copy(
                    src_ref=src, dst_ref=dst, send_sem=s_y.at[d - 1, h], recv_sem=rsem,
                    device_id=(s + 32 * d, x), device_id_type=MESH,
                )
                pl.when(cond & where)(copy.start)
                passes.append((cond & where, copy))

            to_line(lax.rem(y, 2) == 0, 1, src, ry.at[h], r_y.at[2])

            @pl.when(cond & (y < 2))
            def _():
                rows = src[...].astype(F32)
                pack[h] = jnp.concatenate([rows[:, 0, 0:8], rows[:, 1, 0:8]], axis=1).astype(BF16)

            to_line(y == 0, 3, pack.at[h], rp.at[0, h], r_y.at[0])
            to_line(y == 0, 2, pack.at[h], rp.at[0, h], r_y.at[0])
            to_line(y == 1, 1, pack.at[h], rp.at[1, h], r_y.at[1])
            to_line(y == 1, 2, pack.at[h], rp.at[1, h], r_y.at[1])

        for h in range(4):
            later = (y < 3) & (g <= h)
            arrived_if(later & (g != h), rv.at[h], r_v.at[h])
            arrived_if(later & (g == h), rv.at[h, 0:7], r_v.at[h])
            pass_on(later, h, rv.at[h])
        for h in range(2):
            arrived_if(upper2, r2.at[h], r_2.at[h])
            pass_on(upper2, h, r2.at[h, :, :, 0:16])
        arrived_if(upper1, r1, r_1)
        for h in (0, 2):
            pass_on(g == h + 1, h, r1.at[:, :, 0:16])

        for b in range(8):
            arrived(pre.at[b], r_pre.at[b])

        def update(w, keys, values, mask=None, first=False, roll=False):
            nb = ROWS // w
            for b0 in range(0, 8, nb):
                at = (slice(b0, b0 + nb), slice(0, w))
                query = pre[b0 : b0 + nb, 0, 0:w].reshape(ROWS, HEAD_DIM)
                scores = dot_t(query, keys) * SCALE
                if mask is not None:
                    scores = jnp.where(mask(b0 * w, scores.shape), scores, NEG)
                peak = jnp.max(scores, axis=1, keepdims=True)
                if first:
                    peak = jnp.broadcast_to(peak, (ROWS, HEAD_DIM))
                else:
                    was = top[at].reshape(ROWS, HEAD_DIM)
                    peak = jnp.maximum(was, peak)
                    keep = jnp.exp2(was - peak)
                weights = jnp.exp2(scores - peak[:, :1])
                total = jnp.sum(weights, axis=1, keepdims=True)
                if roll:
                    weights = pltpu.roll(weights, 8, axis=1)
                numer = dot(weights.astype(BF16), values)
                if first:
                    total = jnp.broadcast_to(total, (ROWS, HEAD_DIM))
                else:
                    total = total + den[at].reshape(ROWS, HEAD_DIM) * keep
                    numer = numer + num[at].reshape(ROWS, HEAD_DIM) * keep
                top[at] = peak.reshape(nb, w, HEAD_DIM)
                den[at] = total.reshape(nb, w, HEAD_DIM)
                num[at] = numer.reshape(nb, w, HEAD_DIM)

        def place(n, w):
            return n // w * ROWS + position(lax.rem(n, w), head)

        def causal(w, start, shape):
            query = start + lax.broadcasted_iota(jnp.int32, shape, 0)
            key = lax.broadcasted_iota(jnp.int32, shape, 1)
            return place(key, w) <= place(query, w)

        def thin(start, shape):
            query = lax.broadcasted_iota(jnp.int32, shape, 0)
            key = lax.broadcasted_iota(jnp.int32, shape, 1)
            return (lax.rem(query, 16) < 8) & (lax.rem(key, 16) < 8)

        def thin_causal(start, shape):
            return thin(start, shape) & causal(16, start, shape)

        def own(n, w):
            return pre[:, n, 0:w].reshape(8 * w, HEAD_DIM)

        update(64, own(1, 64), own(2, 64), functools.partial(causal, 64), first=True)
        update(32, own(1, 32), own(2, 32), functools.partial(causal, 32))
        update(16, own(1, 16), own(2, 16), functools.partial(causal, 16))
        update(16, own(1, 16), own(2, 16), thin_causal)

        def level_rows(ref, n, w, rows):
            return ref[..., n, 0:w, :].reshape(rows, HEAD_DIM)

        @pl.when(upper1)
        def _():
            update(64, level_rows(r1, 0, 64, 512), level_rows(r1, 1, 64, 512))
            update(32, level_rows(r1, 0, 32, 256), level_rows(r1, 1, 32, 256))
            keys, values = level_rows(r1, 0, 16, 128), level_rows(r1, 1, 16, 128)
            update(16, keys, values)
            update(16, keys, values, thin)

        @pl.when(upper2)
        def _():
            update(32, level_rows(r2, 0, 32, 512), level_rows(r2, 1, 32, 512))
            keys, values = level_rows(r2, 0, 16, 256), level_rows(r2, 1, 16, 256)
            update(16, keys, values)
            update(16, keys, values, thin)

        @pl.when(y >= 2)
        def _():
            for t in range(2):
                arrived(rp.at[t], r_y.at[t])
            both = rp[...].reshape(1024, HEAD_DIM)
            update(16, both, both, thin, roll=True)

        @pl.when(lax.rem(y, 2) == 1)
        def _():
            arrived(ry, r_y.at[2])
            keys, values = ry[:, :, 0].reshape(512, HEAD_DIM), ry[:, :, 1].reshape(512, HEAD_DIM)
            update(16, keys, values)
            update(16, keys, values, thin)

        for b in range(8):
            arrived(l0.at[b], r_l0.at[b])
            peak, total = l0[b, 1, :, 0:1], l0[b, 1, :, 64:65]
            was = top[b]
            best = jnp.maximum(was, peak)
            keep, gain = jnp.exp2(was - best), jnp.exp2(peak - best)
            numer = num[b] * keep + l0[b, 0] * gain
            total = den[b] * keep + total * gain
            ao[b] = (numer / total).astype(BF16)
            send_back(b, 0)
        for b in range(8):
            wait_back(b, 0)

        for cond, copy in passes:
            pl.when(cond)(copy.wait_send)

    for j in range(LOCAL_HEADS):
        for half in range(2):
            sender = 2 * j + (1 - half)
            pl.when(me != sender)(
                functools.partial(arrived, att.at[j, 64 * half : 64 * half + 64], r_att.at[j, half])
            )
        pick = jnp.where(row == position(lane, LOCAL_HEADS * x + j), 1.0, 0.0).astype(BF16)
        nat[:, j * HEAD_DIM : (j + 1) * HEAD_DIM] = dot(pick, att[j]).astype(BF16)

    def quarter(x_):
        return pl.ds(pl.multiple_of(32 * x_, 32), 32)

    for d in (2, 1, 3):
        there = lax.rem(x + d, X)
        send(None, nat.at[quarter(there)], ax.at[x], s_ax.at[d - 1], r_ax.at[d - 1], s, there)

    pl.when(core0)(functools.partial(take_theirs, 2))

    for d in (0, 1, 3, 2):
        there = lax.rem(x + X - d, X)
        if d == 0:
            rows = nat[quarter(x)]
        else:
            arrived(ax.at[there], r_ax.at[d - 1])
            rows = ax[there]
            n = {1: 0, 3: 1, 2: 2}[d]
            pl.when(core1)(functools.partial(arrived, w_ref.at[there], r_ws.at[n]))
        for n in range(D // COLS):
            cols = slice(n * COLS, (n + 1) * COLS)
            product = dot(rows, w_ref[there, :, cols])
            if d > 0:
                product = product + part[:, cols]
            if d == 2:
                o_ref[:, cols] = product.astype(BF16)
            else:
                part[:, cols] = product
    @pl.when(core0)
    def _():
        for m in range(2):
            own_copy(m, 0).wait_send()
            own_copy(m, 1).wait_send()
            far_copy(m).wait_send()
            for n in range(3):
                line_copy(n, m).wait_send()
                share_mine(n, m).wait_send()
                share_theirs(n, m).wait_send()

    for cond, copy in sends:
        if cond is None:
            copy.wait_send()
        else:
            pl.when(cond)(copy.wait_send)

def per_device(query_rows, key_rows, value_rows, out_weight):
    vmem = pl.BlockSpec(memory_space=pltpu.VMEM)
    dma = pltpu.SemaphoreType.DMA
    hd = HEAD_DIM
    return pl.pallas_call(
        kernel,
        out_shape=jax.ShapeDtypeStruct((ROWS // X, D), BF16),
        in_specs=[pl.BlockSpec(memory_space=pl.ANY)] * 4,
        out_specs=vmem,
        scratch_shapes=[
            pltpu.VMEM((ROWS, LOCAL_HEADS * hd), BF16),
            pltpu.VMEM((ROWS, LOCAL_HEADS * hd), BF16),
            pltpu.VMEM((ROWS, LOCAL_HEADS * hd), BF16),
            pltpu.VMEM((LOCAL_HEADS, 3, ROWS, hd), BF16),
            pltpu.VMEM((8, 3, ROWS, hd), BF16),
            pltpu.VMEM((8, 3, 64, hd), BF16),
            pltpu.VMEM((8, 2, 64, hd), BF16),
            pltpu.VMEM((2, 8, 2, 32, hd), BF16),
            pltpu.VMEM((4, 8, 2, 16, hd), BF16),
            pltpu.VMEM((4, 8, 2, 16, hd), BF16),
            pltpu.VMEM((2, 4, 8, 16, hd), BF16),
            pltpu.VMEM((4, 8, 16, hd), BF16),
            pltpu.VMEM((8, 2, 64, hd), F32),
            pltpu.VMEM((8, 2, 64, hd), F32),
            pltpu.VMEM((8, 64, hd), F32),
            pltpu.VMEM((8, 64, hd), F32),
            pltpu.VMEM((8, 64, hd), F32),
            pltpu.VMEM((8, 64, hd), BF16),
            pltpu.VMEM((LOCAL_HEADS, ROWS, hd), BF16),
            pltpu.VMEM((ROWS, LOCAL_HEADS * hd), BF16),
            pltpu.VMEM((X, ROWS // X, LOCAL_HEADS * hd), BF16),
            pltpu.VMEM((X, LOCAL_HEADS * hd, D), BF16),
            pltpu.VMEM((ROWS // X, D), F32),
            pltpu.SemaphoreType.REGULAR,
            dma((3,)), dma, dma((4,)), dma((2, 4)), dma((4, 4)), dma((2, 4)), dma((8,)), dma((3, 4)),
            dma((8,)), dma((8,)), dma((X - 1,)), dma((2, 2)), dma((2,)), dma((3, 2)), dma((3, 4)),
            dma((2, 8)), dma((8,)), dma, dma((2,)), dma((4,)), dma((3,)), dma((8,)), dma((4, 2)),
            dma((X - 1,)), dma((2, 2)), dma((2,)), dma((3, 2)), dma((3,)),
        ],
        compiler_params=pltpu.CompilerParams(
            collective_id=0, has_side_effects=True, vmem_limit_bytes=60 * 1024 * 1024
        ),
    )(query_rows, key_rows, value_rows, out_weight)

def solution(mesh):
    in_specs = (P("seq", "head"), P("seq", "head"), P("seq", "head"), P("head", None))
    return jax.shard_map(
        per_device, mesh=mesh, in_specs=in_specs, out_specs=P(("seq", "head"), None), check_vma=False
    )
```

```python
import functools
import math

import jax
import jax.numpy as jnp
from jax import lax
from jax.experimental import pallas as pl
from jax.experimental.pallas import tpu as pltpu
from jax.sharding import PartitionSpec as P

HEAD_DIM = 128
ROWS = 128
LOCAL_HEADS = 4
X = 4
D = 2048
COLS = D // 4
CHUNK = 128
NEG = -1e30
MESH = pl.DeviceIdType.MESH
F32, BF16 = jnp.float32, jnp.bfloat16
SCALE = math.log2(math.e) / math.sqrt(HEAD_DIM)

def dot(a, b):
    return lax.dot_general(a, b, (((1,), (0,)), ((), ())), preferred_element_type=F32)

def dot_t(a, b):
    return lax.dot_general(a, b, (((1,), (1,)), ((), ())), preferred_element_type=F32)

def position(r, h):
    return jnp.where(
        r < 8,
        lax.rem(h, 16) + 16 * r,
        jnp.where(
            r < 16,
            lax.rem(h + 8, 16) + 16 * (r - 8),
            jnp.where(
                r < 32,
                lax.rem(h + 4, 8) + 8 * (r - 16),
                jnp.where(r < 64, lax.rem(h + 2, 4) + 4 * (r - 32), lax.rem(h + 1, 2) + 2 * (r - 64)),
            ),
        ),
    )

def kernel(
    q_hbm, k_hbm, v_hbm, w_hbm, o_ref,
    q_ref, k_ref, v_ref, perm, blocks, pre, r1, r2, rv, ry, rp, pack, l0, stat, top, den, num, ao, att, nat, ax, w_ref, part,
    go, s_in, s_w, s_p1, s_p2, s_pv, s_blk, s_fwd, s_y, s_l0, s_ret, s_ax, s_wx, s_wf, s_wy, s_ws,
    r_blk, r_pre, r_1, r_2, r_v, r_y, r_l0, r_att, r_ax, r_wx, r_wf, r_wy, r_ws,
):
    s, x = lax.axis_index("seq"), lax.axis_index("head")
    c, i, g, y = lax.rem(s, 2), lax.rem(s // 2, 4), lax.rem(s // 8, 4), s // 32
    me = 2 * i + c
    base = s - me

    line = y * 32
    s_up, s_down = lax.rem(s + 32, 128), lax.rem(s + 96, 128)
    upper1, upper2 = lax.rem(g, 2) == 1, g >= 2
    lower1, lower2 = lax.rem(g, 2) == 0, g < 2
    core0, core1 = c == 0, c == 1

    loads = [
        pltpu.make_async_copy(src, dst, s_in.at[n])
        for n, (src, dst) in enumerate(((q_hbm, q_ref), (k_hbm, k_ref), (v_hbm, v_ref)))
    ]
    for load in loads:
        load.start()
    w_copy = pltpu.make_async_copy(w_hbm, w_ref.at[x], s_w)
    w_copy.start()

    barrier = pltpu.get_barrier_semaphore()

    def greet(s_, x_):
        pl.semaphore_signal(barrier, inc=1, device_id=(s_, x_), device_id_type=MESH)

    @pl.when(core0)
    def _():
        for n in range(0, 8, 2):
            pl.when(me != n)(functools.partial(greet, base + n, x))
        greet(s_up, x)
        greet(s_down, x)

    @pl.when(core1)
    def _():
        for n in range(0, 8, 2):
            greet(base + n, x)
        for d in range(1, 4):
            for n in range(1, 8, 2):
                greet(line + 8 * lax.rem(g + d, 4) + n, x)
            greet(lax.rem(s + 32 * d, 128), x)

    for d in range(1, X):
        greet(s, lax.rem(x + d, X))

    for load in loads:
        load.wait()
    row = lax.broadcasted_iota(jnp.int32, (ROWS, ROWS), 0)
    lane = lax.broadcasted_iota(jnp.int32, (ROWS, ROWS), 1)
    for j in range(LOCAL_HEADS):
        cols = slice(j * HEAD_DIM, (j + 1) * HEAD_DIM)
        pick = jnp.where(lane == position(row, LOCAL_HEADS * x + j), 1.0, 0.0).astype(BF16)
        for n, ref in enumerate((q_ref, k_ref, v_ref)):
            perm[j, n] = dot(pick, ref[:, cols]).astype(BF16)

    @pl.when(core0)
    def _():
        pl.semaphore_wait(barrier, 12)
        for n in range(1, 8, 2):
            pl.semaphore_signal(go, inc=1, device_id=(base + n, x), device_id_type=MESH)

    @pl.when(core1)
    def _():
        pl.semaphore_wait(go, 4)

    sends = []

    def send(cond, src, dst, ssem, rsem, s_, x_=None):
        copy = pltpu.make_async_remote_copy(
            src_ref=src, dst_ref=dst, send_sem=ssem, recv_sem=rsem,
            device_id=(s_, x if x_ is None else x_), device_id_type=MESH,
        )
        sends.append((cond, copy))
        if cond is None:
            copy.start()
        else:
            pl.when(cond)(copy.start)

    def arrived(ref, sem):
        pltpu.make_async_copy(ref, ref, sem).wait()

    def regroup(cond, parts):
        for n in parts:
            part_rows = slice(64 * n, 64 * n + 64)
            for j in range(LOCAL_HEADS):
                send(
                    cond & (me != 2 * j), perm.at[j, :, part_rows], blocks.at[me, :, part_rows],
                    s_blk.at[n, j], r_blk.at[n, me], base + 2 * j,
                )

    regroup(g < 4, (0,))
    regroup(g < 2, (1,))

    x_left, x_right, x_far = lax.rem(x + 3, X), lax.rem(x + 1, X), lax.rem(x + 2, X)
    around = (x_left, x_right, x_far)
    mine = 2 * lax.rem(y, 2)
    theirs = 2 - mine
    w_copy.wait()

    def weight(x_, k):
        return w_ref.at[x_, pl.ds(pl.multiple_of(k * CHUNK, CHUNK), CHUNK)]

    def weight_copy(x_, k, s_, to, ssem, rsem):
        return pltpu.make_async_remote_copy(
            src_ref=weight(x_, k), dst_ref=weight(x_, k), send_sem=ssem, recv_sem=rsem,
            device_id=(s_, to), device_id_type=MESH,
        )

    def own_copy(m, side):
        to = (x_right, x_left)[side]
        return weight_copy(x, mine + m, s, to, s_wx.at[side, m], r_wx.at[side, m])

    def far_copy(m):
        to = (x_right, x_left)[m]
        return weight_copy(around[m], mine + m, s, to, s_wf.at[m], r_wf.at[m])

    def line_copy(n, m):
        to = (s_up, s_down)[m]
        return weight_copy(around[n], mine + m, to, x, s_wy.at[n, m], r_wy.at[n, m])

    def share_mine(n, m):
        return weight_copy(around[n], mine + m, s + 1, x, s_ws.at[n, m], r_ws.at[n])

    def share_theirs(n, m):
        return weight_copy(around[n], theirs + m, s + 1, x, s_ws.at[n, 2 + m], r_ws.at[n])

    def take_theirs(n):
        for m in range(2):
            arrived(weight(around[n], theirs + m), r_wy.at[n, m])
            share_theirs(n, m).start()

    @pl.when(core0)
    def _():
        for m in range(2):
            own_copy(m, 0).start()
            own_copy(1 - m, 1).start()

    @pl.when(core1)
    def _():
        pl.semaphore_wait(barrier, 18)
        pl.semaphore_signal(go, inc=1, device_id=(s - 1, x), device_id_type=MESH)

    @pl.when(core0)
    def _():
        pl.semaphore_wait(go, 1)

    for h in range(4):
        for j in range(LOCAL_HEADS):
            cond = (y < 3) & ((g >= h) | (lower1 & (g + 1 == h))) & ((g != h) | (me != 2 * j + 1))
            send(cond, perm.at[j, 1:3, 0:16], rv.at[g, me], s_pv.at[h, j], r_v.at[g], line + 8 * h + 2 * j + 1)

    rv_sends = sends[-16:]
    for cond, copy in rv_sends:
        pl.when((g > 0) & cond)(copy.wait_send)
    sends[-16:] = [((g == 0) & cond, copy) for cond, copy in rv_sends]
    @pl.when((y < 3) & core1)
    def _():
        rv[g, me] = perm[i, 1:3, 0:16]

    for h in range(2):
        for j in range(LOCAL_HEADS):
            send(
                lower2, perm.at[j, 1:3, 0:32], r2.at[g, me], s_p2.at[h, j], r_2.at[g],
                line + 8 * (2 + h) + 2 * j + 1,
            )
    for j in range(LOCAL_HEADS):
        send(lower1, perm.at[j, 1:3, 0:64], r1.at[me], s_p1.at[j], r_1, base + 8 + 2 * j + 1)
    regroup(g >= 2, (1,))

    head = LOCAL_HEADS * x + i

    def send_back(b, lo):
        there = base + b
        pl.when(me != b)(
            pltpu.make_async_remote_copy(
                src_ref=ao.at[b], dst_ref=att.at[i, lo : lo + 64], send_sem=s_ret.at[b],
                recv_sem=r_att.at[i, lo // 64], device_id=(there, x), device_id_type=MESH,
            ).start
        )

        @pl.when(me == b)
        def _():
            att[i, lo : lo + 64] = ao[b]

    def wait_back(b, lo):
        pl.when(me != b)(
            pltpu.make_async_remote_copy(
                src_ref=ao.at[b], dst_ref=att.at[i, lo : lo + 64], send_sem=s_ret.at[b],
                recv_sem=r_att.at[i, lo // 64], device_id=(base + b, x), device_id_type=MESH,
            ).wait_send
        )

    @pl.when(core0)
    def _():
        blocks[me] = perm[i]

        def forward(b):
            return pltpu.make_async_remote_copy(
                src_ref=blocks.at[b, :, 0:64], dst_ref=pre.at[b], send_sem=s_fwd.at[b], recv_sem=r_pre.at[b],
                device_id=(s + 1, x), device_id_type=MESH,
            )

        def hand(b):
            return pltpu.make_async_remote_copy(
                src_ref=stat.at[b], dst_ref=l0.at[b], send_sem=s_l0.at[b], recv_sem=r_l0.at[b],
                device_id=(s + 1, x), device_id_type=MESH,
            )

        for side in range(2):
            m = side
            arrived(weight(around[side], mine + m), r_wx.at[side, m])
            far_copy(m).start()
            line_copy(side, m).start()
            share_mine(side, m).start()

        for b in range(8):
            pl.when(me != b)(functools.partial(arrived, blocks.at[b, :, 0:64], r_blk.at[0, b]))
            forward(b).start()
        for side in range(2):
            m = 1 - side
            arrived(weight(around[side], mine + m), r_wx.at[side, m])
            line_copy(side, m).start()
            share_mine(side, m).start()

        for m in range(2):
            arrived(weight(x_far, mine + m), r_wf.at[m])
            line_copy(2, m).start()
            share_mine(2, m).start()
        same = position(lane, head) <= position(row, head)
        half = lax.broadcasted_iota(jnp.int32, (64, ROWS), 1) < 64
        for b in range(8):
            pl.when(me != b)(functools.partial(arrived, blocks.at[b, :, 64:128], r_blk.at[1, b]))
            width = ROWS * (b + 1)
            keys = blocks[0 : b + 1, 1].reshape(width, HEAD_DIM)
            values = blocks[0 : b + 1, 2].reshape(width, HEAD_DIM)
            scores = dot_t(blocks[b, 0], keys) * SCALE
            last = jnp.where(same, scores[:, ROWS * b :], NEG)
            scores = last if b == 0 else jnp.concatenate([scores[:, : ROWS * b], last], axis=1)
            peak = jnp.max(scores, axis=1, keepdims=True)
            weights = jnp.exp2(scores - peak)
            total = jnp.sum(weights, axis=1, keepdims=True)
            numer = dot(weights.astype(BF16), values)
            stat[b, 0] = numer[:64]
            stat[b, 1] = jnp.where(half, peak[:64], total[:64])
            hand(b).start()
            ao[b] = (numer[64:] / total[64:]).astype(BF16)
            send_back(b, 64)
        take_theirs(0)
        take_theirs(1)

        for b in range(8):
            forward(b).wait_send()
            hand(b).wait_send()
            wait_back(b, 64)

    @pl.when(core1)
    def _():
        def arrived_if(cond, ref, sem):
            pl.when(cond)(functools.partial(arrived, ref, sem))

        passes = []

        def pass_on(cond, h, src):
            def to_line(where, d, src, dst, rsem):
                copy = pltpu.make_async_remote_copy(
                    src_ref=src, dst_ref=dst, send_sem=s_y.at[d - 1, h], recv_sem=rsem,
                    device_id=(s + 32 * d, x), device_id_type=MESH,
                )
                pl.when(cond & where)(copy.start)
                passes.append((cond & where, copy))

            to_line(lax.rem(y, 2) == 0, 1, src, ry.at[h], r_y.at[2])

            @pl.when(cond & (y < 2))
            def _():
                rows = src[...].astype(F32)
                pack[h] = jnp.concatenate([rows[:, 0, 0:8], rows[:, 1, 0:8]], axis=1).astype(BF16)

            to_line(y == 0, 3, pack.at[h], rp.at[0, h], r_y.at[0])
            to_line(y == 0, 2, pack.at[h], rp.at[0, h], r_y.at[0])
            to_line(y == 1, 1, pack.at[h], rp.at[1, h], r_y.at[1])
            to_line(y == 1, 2, pack.at[h], rp.at[1, h], r_y.at[1])

        for h in range(4):
            later = (y < 3) & ((g <= h) | (upper1 & (g == h + 1)))
            arrived_if(later & (g != h), rv.at[h], r_v.at[h])
            arrived_if(later & (g == h), rv.at[h, 0:7], r_v.at[h])
            pass_on(later, h, rv.at[h])
        for h in range(2):
            arrived_if(upper2, r2.at[h], r_2.at[h])
            pass_on(upper2, h, r2.at[h, :, :, 0:16])

        for b in range(8):
            arrived(pre.at[b], r_pre.at[b])

        def update(w, keys, values, mask=None, first=False, roll=False):
            nb = ROWS // w
            for b0 in range(0, 8, nb):
                at = (slice(b0, b0 + nb), slice(0, w))
                query = pre[b0 : b0 + nb, 0, 0:w].reshape(ROWS, HEAD_DIM)
                scores = dot_t(query, keys) * SCALE
                if mask is not None:
                    scores = jnp.where(mask(b0 * w, scores.shape), scores, NEG)
                peak = jnp.max(scores, axis=1, keepdims=True)
                if first:
                    peak = jnp.broadcast_to(peak, (ROWS, HEAD_DIM))
                else:
                    was = top[at].reshape(ROWS, HEAD_DIM)
                    peak = jnp.maximum(was, peak)
                    keep = jnp.exp2(was - peak)
                weights = jnp.exp2(scores - peak[:, :1])
                total = jnp.sum(weights, axis=1, keepdims=True)
                if roll:
                    weights = pltpu.roll(weights, 8, axis=1)
                numer = dot(weights.astype(BF16), values)
                if first:
                    total = jnp.broadcast_to(total, (ROWS, HEAD_DIM))
                else:
                    total = total + den[at].reshape(ROWS, HEAD_DIM) * keep
                    numer = numer + num[at].reshape(ROWS, HEAD_DIM) * keep
                top[at] = peak.reshape(nb, w, HEAD_DIM)
                den[at] = total.reshape(nb, w, HEAD_DIM)
                num[at] = numer.reshape(nb, w, HEAD_DIM)

        def place(n, w):
            return n // w * ROWS + position(lax.rem(n, w), head)

        def causal(w, start, shape):
            query = start + lax.broadcasted_iota(jnp.int32, shape, 0)
            key = lax.broadcasted_iota(jnp.int32, shape, 1)
            return place(key, w) <= place(query, w)

        def thin(start, shape):
            query = lax.broadcasted_iota(jnp.int32, shape, 0)
            key = lax.broadcasted_iota(jnp.int32, shape, 1)
            return (lax.rem(query, 16) < 8) & (lax.rem(key, 16) < 8)

        def thin_causal(start, shape):
            return thin(start, shape) & causal(16, start, shape)

        def own(n, w):
            return pre[:, n, 0:w].reshape(8 * w, HEAD_DIM)

        update(64, own(1, 64), own(2, 64), functools.partial(causal, 64), first=True)
        update(32, own(1, 32), own(2, 32), functools.partial(causal, 32))
        update(16, own(1, 16), own(2, 16), functools.partial(causal, 16))
        update(16, own(1, 16), own(2, 16), thin_causal)

        def level_rows(ref, n, w, rows):
            return ref[..., n, 0:w, :].reshape(rows, HEAD_DIM)

        @pl.when(upper2)
        def _():
            update(32, level_rows(r2, 0, 32, 512), level_rows(r2, 1, 32, 512))
            keys, values = level_rows(r2, 0, 16, 256), level_rows(r2, 1, 16, 256)
            update(16, keys, values)
            update(16, keys, values, thin)

        arrived_if(upper1, r1, r_1)

        @pl.when(upper1)
        def _():
            update(64, level_rows(r1, 0, 64, 512), level_rows(r1, 1, 64, 512))
            update(32, level_rows(r1, 0, 32, 256), level_rows(r1, 1, 32, 256))
            keys, values = level_rows(r1, 0, 16, 128), level_rows(r1, 1, 16, 128)
            update(16, keys, values)
            update(16, keys, values, thin)

        @pl.when(y >= 2)
        def _():
            for t in range(2):
                arrived(rp.at[t], r_y.at[t])
            both = rp[...].reshape(1024, HEAD_DIM)
            update(16, both, both, thin, roll=True)

        @pl.when(lax.rem(y, 2) == 1)
        def _():
            arrived(ry, r_y.at[2])
            keys, values = ry[:, :, 0].reshape(512, HEAD_DIM), ry[:, :, 1].reshape(512, HEAD_DIM)
            update(16, keys, values)
            update(16, keys, values, thin)

        for b in range(8):
            arrived(l0.at[b], r_l0.at[b])
            peak, total = l0[b, 1, :, 0:1], l0[b, 1, :, 64:65]
            was = top[b]
            best = jnp.maximum(was, peak)
            keep, gain = jnp.exp2(was - best), jnp.exp2(peak - best)
            numer = num[b] * keep + l0[b, 0] * gain
            total = den[b] * keep + total * gain
            ao[b] = (numer / total).astype(BF16)
            send_back(b, 0)
        for b in range(8):
            wait_back(b, 0)

        for cond, copy in passes:
            pl.when(cond)(copy.wait_send)

    def quarter(x_):
        return pl.ds(pl.multiple_of(32 * x_, 32), 32)

    for j in range(LOCAL_HEADS):
        for half in range(2):
            sender = 2 * j + (1 - half)
            pl.when(me != sender)(
                functools.partial(arrived, att.at[j, 64 * half : 64 * half + 64], r_att.at[j, half])
            )
        pick = jnp.where(row == position(lane, LOCAL_HEADS * x + j), 1.0, 0.0).astype(BF16)
        nat[j] = dot(pick, att[j]).astype(BF16)
        for d in (2, 1, 3):
            there = lax.rem(x + d, X)
            send(None, nat.at[j, quarter(there)], ax.at[x, j], s_ax.at[d - 1, j], r_ax.at[d - 1], s, there)

    pl.when(core0)(functools.partial(take_theirs, 2))

    for d in (0, 1, 3, 2):
        there = lax.rem(x + X - d, X)
        if d == 0:
            rows = nat[:, quarter(x)]
        else:
            arrived(ax.at[there], r_ax.at[d - 1])
            rows = ax[there]
            n = {1: 0, 3: 1, 2: 2}[d]
            pl.when(core1)(functools.partial(arrived, w_ref.at[there], r_ws.at[n]))
        rows = jnp.concatenate([rows[j] for j in range(LOCAL_HEADS)], axis=1)
        for n in range(D // COLS):
            cols = slice(n * COLS, (n + 1) * COLS)
            product = dot(rows, w_ref[there, :, cols])
            if d > 0:
                product = product + part[:, cols]
            if d == 2:
                o_ref[:, cols] = product.astype(BF16)
            else:
                part[:, cols] = product
    @pl.when(core0)
    def _():
        for m in range(2):
            own_copy(m, 0).wait_send()
            own_copy(m, 1).wait_send()
            far_copy(m).wait_send()
            for n in range(3):
                line_copy(n, m).wait_send()
                share_mine(n, m).wait_send()
                share_theirs(n, m).wait_send()

    for cond, copy in sends:
        if cond is None:
            copy.wait_send()
        else:
            pl.when(cond)(copy.wait_send)

def per_device(query_rows, key_rows, value_rows, out_weight):
    vmem = pl.BlockSpec(memory_space=pltpu.VMEM)
    dma = pltpu.SemaphoreType.DMA
    hd = HEAD_DIM
    return pl.pallas_call(
        kernel,
        out_shape=jax.ShapeDtypeStruct((ROWS // X, D), BF16),
        in_specs=[pl.BlockSpec(memory_space=pl.ANY)] * 4,
        out_specs=vmem,
        scratch_shapes=[
            pltpu.VMEM((ROWS, LOCAL_HEADS * hd), BF16),
            pltpu.VMEM((ROWS, LOCAL_HEADS * hd), BF16),
            pltpu.VMEM((ROWS, LOCAL_HEADS * hd), BF16),
            pltpu.VMEM((LOCAL_HEADS, 3, ROWS, hd), BF16),
            pltpu.VMEM((8, 3, ROWS, hd), BF16),
            pltpu.VMEM((8, 3, 64, hd), BF16),
            pltpu.VMEM((8, 2, 64, hd), BF16),
            pltpu.VMEM((2, 8, 2, 32, hd), BF16),
            pltpu.VMEM((4, 8, 2, 16, hd), BF16),
            pltpu.VMEM((4, 8, 2, 16, hd), BF16),
            pltpu.VMEM((2, 4, 8, 16, hd), BF16),
            pltpu.VMEM((4, 8, 16, hd), BF16),
            pltpu.VMEM((8, 2, 64, hd), F32),
            pltpu.VMEM((8, 2, 64, hd), F32),
            pltpu.VMEM((8, 64, hd), F32),
            pltpu.VMEM((8, 64, hd), F32),
            pltpu.VMEM((8, 64, hd), F32),
            pltpu.VMEM((8, 64, hd), BF16),
            pltpu.VMEM((LOCAL_HEADS, ROWS, hd), BF16),
            pltpu.VMEM((LOCAL_HEADS, ROWS, hd), BF16),
            pltpu.VMEM((X, LOCAL_HEADS, ROWS // X, hd), BF16),
            pltpu.VMEM((X, LOCAL_HEADS * hd, D), BF16),
            pltpu.VMEM((ROWS // X, D), F32),
            pltpu.SemaphoreType.REGULAR,
            dma((3,)), dma, dma((4,)), dma((2, 4)), dma((4, 4)), dma((2, 4)), dma((8,)), dma((3, 4)),
            dma((8,)), dma((8,)), dma((X - 1, 4)), dma((2, 2)), dma((2,)), dma((3, 2)), dma((3, 4)),
            dma((2, 8)), dma((8,)), dma, dma((2,)), dma((4,)), dma((3,)), dma((8,)), dma((4, 2)),
            dma((X - 1,)), dma((2, 2)), dma((2,)), dma((3, 2)), dma((3,)),
        ],
        compiler_params=pltpu.CompilerParams(
            collective_id=0, has_side_effects=True, vmem_limit_bytes=60 * 1024 * 1024
        ),
    )(query_rows, key_rows, value_rows, out_weight)

def solution(mesh):
    in_specs = (P("seq", "head"), P("seq", "head"), P("seq", "head"), P("head", None))
    return jax.shard_map(
        per_device, mesh=mesh, in_specs=in_specs, out_specs=P(("seq", "head"), None), check_vma=False
    )
```

```python
import functools
import math

import jax
import jax.numpy as jnp
from jax import lax
from jax.experimental import pallas as pl
from jax.experimental.pallas import tpu as pltpu
from jax.sharding import PartitionSpec as P

HEAD_DIM = 128
ROWS = 128
LOCAL_HEADS = 4
X = 4
D = 2048
COLS = D // 4
CHUNK = 128
NEG = -1e30
MESH = pl.DeviceIdType.MESH
F32, BF16 = jnp.float32, jnp.bfloat16
SCALE = math.log2(math.e) / math.sqrt(HEAD_DIM)

def dot(a, b):
    return lax.dot_general(a, b, (((1,), (0,)), ((), ())), preferred_element_type=F32)

def dot_t(a, b):
    return lax.dot_general(a, b, (((1,), (1,)), ((), ())), preferred_element_type=F32)

def levels(r):
    return sum(jnp.where(r < n, 1, 0) for n in (64, 32, 16, 8))


def position(r, h):
    return jnp.where(
        r < 8,
        lax.rem(h, 16) + 16 * r,
        jnp.where(
            r < 16,
            lax.rem(h + 8, 16) + 16 * (r - 8),
            jnp.where(
                r < 32,
                lax.rem(h + 4, 8) + 8 * (r - 16),
                jnp.where(r < 64, lax.rem(h + 2, 4) + 4 * (r - 32), lax.rem(h + 1, 2) + 2 * (r - 64)),
            ),
        ),
    )

def kernel(
    q_hbm, k_hbm, v_hbm, w_hbm, o_ref,
    q_ref, k_ref, v_ref, perm, blocks, pre, r1, r2, rv, ry, rp, pack, l0, stat, top, den, num, ao, att, nat, ax, w_ref, part,
    go, s_in, s_w, s_p1, s_p2, s_pv, s_blk, s_fwd, s_y, s_l0, s_ret, s_ax, s_wx, s_wf, s_wy, s_ws,
    r_blk, r_pre, r_1, r_2, r_v, r_y, r_l0, r_att, r_ax, r_wx, r_wf, r_wy, r_ws,
):
    s, x = lax.axis_index("seq"), lax.axis_index("head")
    c, i, g, y = lax.rem(s, 2), lax.rem(s // 2, 4), lax.rem(s // 8, 4), s // 32
    me = 2 * i + c
    base = s - me

    line = y * 32
    s_up, s_down = lax.rem(s + 32, 128), lax.rem(s + 96, 128)
    upper1, upper2 = lax.rem(g, 2) == 1, g >= 2
    lower1, lower2 = lax.rem(g, 2) == 0, g < 2
    core0, core1 = c == 0, c == 1

    loads = [
        pltpu.make_async_copy(src, dst, s_in.at[n])
        for n, (src, dst) in enumerate(((q_hbm, q_ref), (k_hbm, k_ref), (v_hbm, v_ref)))
    ]
    for load in loads:
        load.start()
    w_copy = pltpu.make_async_copy(w_hbm, w_ref.at[x], s_w)
    w_copy.start()

    barrier = pltpu.get_barrier_semaphore()

    def greet(s_, x_):
        pl.semaphore_signal(barrier, inc=1, device_id=(s_, x_), device_id_type=MESH)

    @pl.when(core0)
    def _():
        for n in range(0, 8, 2):
            pl.when(me != n)(functools.partial(greet, base + n, x))
        greet(s_up, x)
        greet(s_down, x)

    @pl.when(core1)
    def _():
        for n in range(0, 8, 2):
            greet(base + n, x)
        for d in range(1, 4):
            for n in range(1, 8, 2):
                greet(line + 8 * lax.rem(g + d, 4) + n, x)
            greet(lax.rem(s + 32 * d, 128), x)

    for d in range(1, X):
        greet(s, lax.rem(x + d, X))

    for load in loads:
        load.wait()
    row = lax.broadcasted_iota(jnp.int32, (ROWS, ROWS), 0)
    lane = lax.broadcasted_iota(jnp.int32, (ROWS, ROWS), 1)
    for j in range(LOCAL_HEADS):
        cols = slice(j * HEAD_DIM, (j + 1) * HEAD_DIM)
        pick = jnp.where(lane == position(row, LOCAL_HEADS * x + j), 1.0, 0.0).astype(BF16)
        for n, ref in enumerate((q_ref, k_ref, v_ref)):
            perm[j, n] = dot(pick, ref[:, cols]).astype(BF16)

    @pl.when(core0)
    def _():
        pl.semaphore_wait(barrier, 12)
        for n in range(1, 8, 2):
            pl.semaphore_signal(go, inc=1, device_id=(base + n, x), device_id_type=MESH)

    @pl.when(core1)
    def _():
        pl.semaphore_wait(go, 4)

    sends = []

    def send(cond, src, dst, ssem, rsem, s_, x_=None):
        copy = pltpu.make_async_remote_copy(
            src_ref=src, dst_ref=dst, send_sem=ssem, recv_sem=rsem,
            device_id=(s_, x if x_ is None else x_), device_id_type=MESH,
        )
        sends.append((cond, copy))
        if cond is None:
            copy.start()
        else:
            pl.when(cond)(copy.start)

    def arrived(ref, sem):
        pltpu.make_async_copy(ref, ref, sem).wait()

    def regroup(cond, parts):
        for n in parts:
            part_rows = slice(64 * n, 64 * n + 64)
            for j in range(LOCAL_HEADS):
                send(
                    cond & (me != 2 * j), perm.at[j, :, part_rows], blocks.at[me, :, part_rows],
                    s_blk.at[n, j], r_blk.at[n, me], base + 2 * j,
                )

    regroup(g < 4, (0,))
    regroup(g < 2, (1,))

    x_left, x_right, x_far = lax.rem(x + 3, X), lax.rem(x + 1, X), lax.rem(x + 2, X)
    around = (x_left, x_right, x_far)
    mine = 2 * lax.rem(y, 2)
    theirs = 2 - mine
    w_copy.wait()

    def weight(x_, k):
        return w_ref.at[x_, pl.ds(pl.multiple_of(k * CHUNK, CHUNK), CHUNK)]

    def weight_copy(x_, k, s_, to, ssem, rsem):
        return pltpu.make_async_remote_copy(
            src_ref=weight(x_, k), dst_ref=weight(x_, k), send_sem=ssem, recv_sem=rsem,
            device_id=(s_, to), device_id_type=MESH,
        )

    def own_copy(m, side):
        to = (x_right, x_left)[side]
        return weight_copy(x, mine + m, s, to, s_wx.at[side, m], r_wx.at[side, m])

    def far_copy(m):
        to = (x_right, x_left)[m]
        return weight_copy(around[m], mine + m, s, to, s_wf.at[m], r_wf.at[m])

    def line_copy(n, m):
        to = (s_up, s_down)[m]
        return weight_copy(around[n], mine + m, to, x, s_wy.at[n, m], r_wy.at[n, m])

    def share_mine(n, m):
        return weight_copy(around[n], mine + m, s + 1, x, s_ws.at[n, m], r_ws.at[n])

    def share_theirs(n, m):
        return weight_copy(around[n], theirs + m, s + 1, x, s_ws.at[n, 2 + m], r_ws.at[n])

    def take_theirs(n):
        for m in range(2):
            arrived(weight(around[n], theirs + m), r_wy.at[n, m])
            share_theirs(n, m).start()

    @pl.when(core0)
    def _():
        for m in range(2):
            own_copy(m, 0).start()
            own_copy(1 - m, 1).start()

    @pl.when(core1)
    def _():
        pl.semaphore_wait(barrier, 18)
        pl.semaphore_signal(go, inc=1, device_id=(s - 1, x), device_id_type=MESH)

    @pl.when(core0)
    def _():
        pl.semaphore_wait(go, 1)

    for h in range(4):
        for j in range(LOCAL_HEADS):
            cond = (y < 3) & ((g >= h) | (lower1 & (g + 1 == h))) & ((g != h) | (me != 2 * j + 1))
            send(cond, perm.at[j, 1:3, 0:16], rv.at[g, me], s_pv.at[h, j], r_v.at[g], line + 8 * h + 2 * j + 1)

    rv_sends = sends[-16:]
    for cond, copy in rv_sends:
        pl.when((g > 0) & cond)(copy.wait_send)
    sends[-16:] = [((g == 0) & cond, copy) for cond, copy in rv_sends]
    @pl.when((y < 3) & core1)
    def _():
        rv[g, me] = perm[i, 1:3, 0:16]

    for h in range(2):
        for j in range(LOCAL_HEADS):
            send(
                lower2, perm.at[j, 1:3, 0:32], r2.at[g, me], s_p2.at[h, j], r_2.at[g],
                line + 8 * (2 + h) + 2 * j + 1,
            )
    for j in range(LOCAL_HEADS):
        send(lower1, perm.at[j, 1:3, 0:64], r1.at[me], s_p1.at[j], r_1, base + 8 + 2 * j + 1)
    regroup(g >= 2, (1,))

    head = LOCAL_HEADS * x + i

    def send_back(b, lo):
        there = base + b
        pl.when(me != b)(
            pltpu.make_async_remote_copy(
                src_ref=ao.at[b], dst_ref=att.at[i, lo : lo + 64], send_sem=s_ret.at[b],
                recv_sem=r_att.at[i, lo // 64], device_id=(there, x), device_id_type=MESH,
            ).start
        )

        @pl.when(me == b)
        def _():
            att[i, lo : lo + 64] = ao[b]

    def wait_back(b, lo):
        pl.when(me != b)(
            pltpu.make_async_remote_copy(
                src_ref=ao.at[b], dst_ref=att.at[i, lo : lo + 64], send_sem=s_ret.at[b],
                recv_sem=r_att.at[i, lo // 64], device_id=(base + b, x), device_id_type=MESH,
            ).wait_send
        )

    @pl.when(core0)
    def _():
        blocks[me] = perm[i]

        def forward(b):
            return pltpu.make_async_remote_copy(
                src_ref=blocks.at[b, 0, 0:64], dst_ref=pre.at[b], send_sem=s_fwd.at[b], recv_sem=r_pre.at[b],
                device_id=(s + 1, x), device_id_type=MESH,
            )

        def hand(b):
            return pltpu.make_async_remote_copy(
                src_ref=stat.at[b], dst_ref=l0.at[b], send_sem=s_l0.at[b], recv_sem=r_l0.at[b],
                device_id=(s + 1, x), device_id_type=MESH,
            )

        for side in range(2):
            m = side
            arrived(weight(around[side], mine + m), r_wx.at[side, m])
            far_copy(m).start()
            line_copy(side, m).start()
            share_mine(side, m).start()

        for b in range(8):
            pl.when(me != b)(functools.partial(arrived, blocks.at[b, :, 0:64], r_blk.at[0, b]))
            forward(b).start()
        for side in range(2):
            m = 1 - side
            arrived(weight(around[side], mine + m), r_wx.at[side, m])
            line_copy(side, m).start()
            share_mine(side, m).start()

        for m in range(2):
            arrived(weight(x_far, mine + m), r_wf.at[m])
            line_copy(2, m).start()
            share_mine(2, m).start()
        same = position(lane, head) <= position(row, head)
        times = (1 + jnp.minimum(levels(row), levels(lane))).astype(F32)
        half = lax.broadcasted_iota(jnp.int32, (64, ROWS), 1) < 64
        for b in range(8):
            pl.when(me != b)(functools.partial(arrived, blocks.at[b, :, 64:128], r_blk.at[1, b]))
            width = ROWS * (b + 1)
            keys = blocks[0 : b + 1, 1].reshape(width, HEAD_DIM)
            values = blocks[0 : b + 1, 2].reshape(width, HEAD_DIM)
            scores = dot_t(blocks[b, 0], keys) * SCALE
            last = jnp.where(same, scores[:, ROWS * b :], NEG)
            scores = last if b == 0 else jnp.concatenate([scores[:, : ROWS * b], last], axis=1)
            peak = jnp.max(scores, axis=1, keepdims=True)
            weights = jnp.exp2(scores - peak) * jnp.concatenate([times] * (b + 1), axis=1)
            total = jnp.sum(weights, axis=1, keepdims=True)
            numer = dot(weights.astype(BF16), values)
            stat[b, 0] = numer[:64]
            stat[b, 1] = jnp.where(half, peak[:64], total[:64])
            hand(b).start()
            ao[b] = (numer[64:] / total[64:]).astype(BF16)
            send_back(b, 64)
        take_theirs(0)
        take_theirs(1)

        for b in range(8):
            forward(b).wait_send()
            hand(b).wait_send()
            wait_back(b, 64)

    @pl.when(core1)
    def _():
        def arrived_if(cond, ref, sem):
            pl.when(cond)(functools.partial(arrived, ref, sem))

        passes = []

        def pass_on(cond, h, src):
            def to_line(where, d, src, dst, rsem):
                copy = pltpu.make_async_remote_copy(
                    src_ref=src, dst_ref=dst, send_sem=s_y.at[d - 1, h], recv_sem=rsem,
                    device_id=(s + 32 * d, x), device_id_type=MESH,
                )
                pl.when(cond & where)(copy.start)
                passes.append((cond & where, copy))

            to_line(lax.rem(y, 2) == 0, 1, src, ry.at[h], r_y.at[2])

            @pl.when(cond & (y < 2))
            def _():
                rows = src[...].astype(F32)
                pack[h] = jnp.concatenate([rows[:, 0, 0:8], rows[:, 1, 0:8]], axis=1).astype(BF16)

            to_line(y == 0, 3, pack.at[h], rp.at[0, h], r_y.at[0])
            to_line(y == 0, 2, pack.at[h], rp.at[0, h], r_y.at[0])
            to_line(y == 1, 1, pack.at[h], rp.at[1, h], r_y.at[1])
            to_line(y == 1, 2, pack.at[h], rp.at[1, h], r_y.at[1])

        for h in range(4):
            later = (y < 3) & ((g <= h) | (upper1 & (g == h + 1)))
            arrived_if(later & (g != h), rv.at[h], r_v.at[h])
            arrived_if(later & (g == h), rv.at[h, 0:7], r_v.at[h])
            pass_on(later, h, rv.at[h])
        for h in range(2):
            arrived_if(upper2, r2.at[h], r_2.at[h])
            pass_on(upper2, h, r2.at[h, :, :, 0:16])

        for b in range(8):
            arrived(pre.at[b], r_pre.at[b])

        top[...] = jnp.full_like(top, NEG)
        den[...] = jnp.zeros_like(den)
        num[...] = jnp.zeros_like(num)

        def update(w, keys, values, packed=False):
            nb = ROWS // w
            shape = (ROWS, keys.shape[0])
            r_query = lax.rem(lax.broadcasted_iota(jnp.int32, shape, 0), w)
            r_key = lax.rem(lax.broadcasted_iota(jnp.int32, shape, 1), w)
            if packed:
                both = (r_query < 8) & (r_key < 8)
                count = jnp.where(both, 1.0, 0.0)
            else:
                count = (jnp.minimum(levels(r_query), levels(r_key)) - {64: 0, 32: 1, 16: 2}[w]).astype(F32)
            for b0 in range(0, 8, nb):
                at = (slice(b0, b0 + nb), slice(0, w))
                query = pre[b0 : b0 + nb, 0:w].reshape(ROWS, HEAD_DIM)
                scores = dot_t(query, keys) * SCALE
                if packed:
                    scores = jnp.where(both, scores, NEG)
                was = top[at].reshape(ROWS, HEAD_DIM)
                peak = jnp.maximum(was, jnp.max(scores, axis=1, keepdims=True))
                keep = jnp.exp2(was - peak)
                weights = jnp.exp2(scores - peak[:, :1]) * count
                total = jnp.sum(weights, axis=1, keepdims=True) + den[at].reshape(ROWS, HEAD_DIM) * keep
                if packed:
                    weights = pltpu.roll(weights, 8, axis=1)
                numer = dot(weights.astype(BF16), values) + num[at].reshape(ROWS, HEAD_DIM) * keep
                top[at] = peak.reshape(nb, w, HEAD_DIM)
                den[at] = total.reshape(nb, w, HEAD_DIM)
                num[at] = numer.reshape(nb, w, HEAD_DIM)

        def level_rows(ref, n, w, rows):
            return ref[..., n, 0:w, :].reshape(rows, HEAD_DIM)

        @pl.when(upper2)
        def _():
            update(32, level_rows(r2, 0, 32, 512), level_rows(r2, 1, 32, 512))

        arrived_if(upper1, r1, r_1)

        @pl.when(upper1)
        def _():
            update(64, level_rows(r1, 0, 64, 512), level_rows(r1, 1, 64, 512))

        @pl.when(y >= 2)
        def _():
            for t in range(2):
                arrived(rp.at[t], r_y.at[t])
            tiles = rp[...].reshape(1024, HEAD_DIM)
            update(16, tiles, tiles, packed=True)

        @pl.when(lax.rem(y, 2) == 1)
        def _():
            arrived(ry, r_y.at[2])
            update(16, ry[:, :, 0].reshape(512, HEAD_DIM), ry[:, :, 1].reshape(512, HEAD_DIM))

        for b in range(8):
            arrived(l0.at[b], r_l0.at[b])
            peak, total = l0[b, 1, :, 0:1], l0[b, 1, :, 64:65]
            was = top[b]
            best = jnp.maximum(was, peak)
            keep, gain = jnp.exp2(was - best), jnp.exp2(peak - best)
            numer = num[b] * keep + l0[b, 0] * gain
            total = den[b] * keep + total * gain
            ao[b] = (numer / total).astype(BF16)
            send_back(b, 0)
        for b in range(8):
            wait_back(b, 0)

        for cond, copy in passes:
            pl.when(cond)(copy.wait_send)

    def quarter(x_):
        return pl.ds(pl.multiple_of(32 * x_, 32), 32)

    for j in range(LOCAL_HEADS):
        for half in range(2):
            sender = 2 * j + (1 - half)
            pl.when(me != sender)(
                functools.partial(arrived, att.at[j, 64 * half : 64 * half + 64], r_att.at[j, half])
            )
        pick = jnp.where(row == position(lane, LOCAL_HEADS * x + j), 1.0, 0.0).astype(BF16)
        nat[j] = dot(pick, att[j]).astype(BF16)
        for d in (2, 1, 3):
            there = lax.rem(x + d, X)
            send(None, nat.at[j, quarter(there)], ax.at[x, j], s_ax.at[d - 1, j], r_ax.at[d - 1], s, there)

    pl.when(core0)(functools.partial(take_theirs, 2))

    for d in (0, 1, 3, 2):
        there = lax.rem(x + X - d, X)
        if d == 0:
            rows = nat[:, quarter(x)]
        else:
            arrived(ax.at[there], r_ax.at[d - 1])
            rows = ax[there]
            n = {1: 0, 3: 1, 2: 2}[d]
            pl.when(core1)(functools.partial(arrived, w_ref.at[there], r_ws.at[n]))
        rows = jnp.concatenate([rows[j] for j in range(LOCAL_HEADS)], axis=1)
        for n in range(D // COLS):
            cols = slice(n * COLS, (n + 1) * COLS)
            product = dot(rows, w_ref[there, :, cols])
            if d > 0:
                product = product + part[:, cols]
            if d == 2:
                o_ref[:, cols] = product.astype(BF16)
            else:
                part[:, cols] = product
    @pl.when(core0)
    def _():
        for m in range(2):
            own_copy(m, 0).wait_send()
            own_copy(m, 1).wait_send()
            far_copy(m).wait_send()
            for n in range(3):
                line_copy(n, m).wait_send()
                share_mine(n, m).wait_send()
                share_theirs(n, m).wait_send()

    for cond, copy in sends:
        if cond is None:
            copy.wait_send()
        else:
            pl.when(cond)(copy.wait_send)

def per_device(query_rows, key_rows, value_rows, out_weight):
    vmem = pl.BlockSpec(memory_space=pltpu.VMEM)
    dma = pltpu.SemaphoreType.DMA
    hd = HEAD_DIM
    return pl.pallas_call(
        kernel,
        out_shape=jax.ShapeDtypeStruct((ROWS // X, D), BF16),
        in_specs=[pl.BlockSpec(memory_space=pl.ANY)] * 4,
        out_specs=vmem,
        scratch_shapes=[
            pltpu.VMEM((ROWS, LOCAL_HEADS * hd), BF16),
            pltpu.VMEM((ROWS, LOCAL_HEADS * hd), BF16),
            pltpu.VMEM((ROWS, LOCAL_HEADS * hd), BF16),
            pltpu.VMEM((LOCAL_HEADS, 3, ROWS, hd), BF16),
            pltpu.VMEM((8, 3, ROWS, hd), BF16),
            pltpu.VMEM((8, 64, hd), BF16),
            pltpu.VMEM((8, 2, 64, hd), BF16),
            pltpu.VMEM((2, 8, 2, 32, hd), BF16),
            pltpu.VMEM((4, 8, 2, 16, hd), BF16),
            pltpu.VMEM((4, 8, 2, 16, hd), BF16),
            pltpu.VMEM((2, 4, 8, 16, hd), BF16),
            pltpu.VMEM((4, 8, 16, hd), BF16),
            pltpu.VMEM((8, 2, 64, hd), F32),
            pltpu.VMEM((8, 2, 64, hd), F32),
            pltpu.VMEM((8, 64, hd), F32),
            pltpu.VMEM((8, 64, hd), F32),
            pltpu.VMEM((8, 64, hd), F32),
            pltpu.VMEM((8, 64, hd), BF16),
            pltpu.VMEM((LOCAL_HEADS, ROWS, hd), BF16),
            pltpu.VMEM((LOCAL_HEADS, ROWS, hd), BF16),
            pltpu.VMEM((X, LOCAL_HEADS, ROWS // X, hd), BF16),
            pltpu.VMEM((X, LOCAL_HEADS * hd, D), BF16),
            pltpu.VMEM((ROWS // X, D), F32),
            pltpu.SemaphoreType.REGULAR,
            dma((3,)), dma, dma((4,)), dma((2, 4)), dma((4, 4)), dma((2, 4)), dma((8,)), dma((3, 4)),
            dma((8,)), dma((8,)), dma((X - 1, 4)), dma((2, 2)), dma((2,)), dma((3, 2)), dma((3, 4)),
            dma((2, 8)), dma((8,)), dma, dma((2,)), dma((4,)), dma((3,)), dma((8,)), dma((4, 2)),
            dma((X - 1,)), dma((2, 2)), dma((2,)), dma((3, 2)), dma((3,)),
        ],
        compiler_params=pltpu.CompilerParams(
            collective_id=0, has_side_effects=True, vmem_limit_bytes=60 * 1024 * 1024
        ),
    )(query_rows, key_rows, value_rows, out_weight)

def solution(mesh):
    in_specs = (P("seq", "head"), P("seq", "head"), P("seq", "head"), P("head", None))
    return jax.shard_map(
        per_device, mesh=mesh, in_specs=in_specs, out_specs=P(("seq", "head"), None), check_vma=False
    )
```

```python
import functools
import math

import jax
import jax.numpy as jnp
from jax import lax
from jax.experimental import pallas as pl
from jax.experimental.pallas import tpu as pltpu
from jax.sharding import PartitionSpec as P

HEAD_DIM = 128
ROWS = 128
LOCAL_HEADS = 4
X = 4
D = 2048
COLS = D // 4
CHUNK = 128
NEG = -1e30
MESH = pl.DeviceIdType.MESH
F32, BF16 = jnp.float32, jnp.bfloat16
SCALE = math.log2(math.e) / math.sqrt(HEAD_DIM)

def dot(a, b):
    return lax.dot_general(a, b, (((1,), (0,)), ((), ())), preferred_element_type=F32)

def dot_t(a, b):
    return lax.dot_general(a, b, (((1,), (1,)), ((), ())), preferred_element_type=F32)

def levels(r):
    return sum(jnp.where(r < n, 1, 0) for n in (64, 32, 16, 8))


def position(r, h):
    return jnp.where(
        r < 8,
        lax.rem(h, 16) + 16 * r,
        jnp.where(
            r < 16,
            lax.rem(h + 8, 16) + 16 * (r - 8),
            jnp.where(
                r < 32,
                lax.rem(h + 4, 8) + 8 * (r - 16),
                jnp.where(r < 64, lax.rem(h + 2, 4) + 4 * (r - 32), lax.rem(h + 1, 2) + 2 * (r - 64)),
            ),
        ),
    )

def kernel(
    q_hbm, k_hbm, v_hbm, w_hbm, o_ref,
    q_ref, k_ref, v_ref, perm, blocks, pre, r1, r2, rv, ry, rp, pack, l0, stat, top, den, num, ao, att, nat, ax, w_ref, part,
    go, s_in, s_w, s_p1, s_p2, s_pv, s_blk, s_fwd, s_y, s_l0, s_ret, s_ax, s_wx, s_wf, s_wy, s_ws,
    r_blk, r_pre, r_1, r_2, r_v, r_y, r_l0, r_att, r_ax, r_wx, r_wf, r_wy, r_ws,
):
    s, x = lax.axis_index("seq"), lax.axis_index("head")
    c, i, g, y = lax.rem(s, 2), lax.rem(s // 2, 4), lax.rem(s // 8, 4), s // 32
    me = 2 * i + c
    base = s - me

    line = y * 32
    s_up, s_down = lax.rem(s + 32, 128), lax.rem(s + 96, 128)
    upper1, upper2 = lax.rem(g, 2) == 1, g >= 2
    lower1, lower2 = lax.rem(g, 2) == 0, g < 2
    core0, core1 = c == 0, c == 1

    loads = [
        pltpu.make_async_copy(src, dst, s_in.at[n])
        for n, (src, dst) in enumerate(((q_hbm, q_ref), (k_hbm, k_ref), (v_hbm, v_ref)))
    ]
    for load in loads:
        load.start()
    w_copy = pltpu.make_async_copy(w_hbm, w_ref.at[x], s_w)
    w_copy.start()

    barrier = pltpu.get_barrier_semaphore()

    def greet(s_, x_):
        pl.semaphore_signal(barrier, inc=1, device_id=(s_, x_), device_id_type=MESH)

    @pl.when(core0)
    def _():
        for n in range(0, 8, 2):
            pl.when(me != n)(functools.partial(greet, base + n, x))
        greet(s_up, x)
        greet(s_down, x)

    @pl.when(core1)
    def _():
        for n in range(0, 8, 2):
            greet(base + n, x)
        for d in range(1, 4):
            for n in range(1, 8, 2):
                greet(line + 8 * lax.rem(g + d, 4) + n, x)
            greet(lax.rem(s + 32 * d, 128), x)

    for d in range(1, X):
        greet(s, lax.rem(x + d, X))

    for load in loads:
        load.wait()
    row = lax.broadcasted_iota(jnp.int32, (ROWS, ROWS), 0)
    lane = lax.broadcasted_iota(jnp.int32, (ROWS, ROWS), 1)
    for j in range(LOCAL_HEADS):
        cols = slice(j * HEAD_DIM, (j + 1) * HEAD_DIM)
        pick = jnp.where(lane == position(row, LOCAL_HEADS * x + j), 1.0, 0.0).astype(BF16)
        for n, ref in enumerate((q_ref, k_ref, v_ref)):
            perm[j, n] = dot(pick, ref[:, cols]).astype(BF16)

    @pl.when(core0)
    def _():
        pl.semaphore_wait(barrier, 12)
        for n in range(1, 8, 2):
            pl.semaphore_signal(go, inc=1, device_id=(base + n, x), device_id_type=MESH)

    @pl.when(core1)
    def _():
        pl.semaphore_wait(go, 4)

    sends = []

    def send(cond, src, dst, ssem, rsem, s_, x_=None):
        copy = pltpu.make_async_remote_copy(
            src_ref=src, dst_ref=dst, send_sem=ssem, recv_sem=rsem,
            device_id=(s_, x if x_ is None else x_), device_id_type=MESH,
        )
        sends.append((cond, copy))
        if cond is None:
            copy.start()
        else:
            pl.when(cond)(copy.start)

    def arrived(ref, sem):
        pltpu.make_async_copy(ref, ref, sem).wait()

    def regroup(cond, parts):
        for n in parts:
            part_rows = slice(64 * n, 64 * n + 64)
            for j in range(LOCAL_HEADS):
                send(
                    cond & (me != 2 * j), perm.at[j, :, part_rows], blocks.at[me, :, part_rows],
                    s_blk.at[n, j], r_blk.at[n, me], base + 2 * j,
                )

    regroup(g < 4, (0,))
    regroup(g < 2, (1,))

    x_left, x_right, x_far = lax.rem(x + 3, X), lax.rem(x + 1, X), lax.rem(x + 2, X)
    around = (x_left, x_right, x_far)
    mine = 2 * lax.rem(y, 2)
    theirs = 2 - mine
    w_copy.wait()

    def weight(x_, k):
        return w_ref.at[x_, pl.ds(pl.multiple_of(k * CHUNK, CHUNK), CHUNK)]

    def weight_copy(x_, k, s_, to, ssem, rsem):
        return pltpu.make_async_remote_copy(
            src_ref=weight(x_, k), dst_ref=weight(x_, k), send_sem=ssem, recv_sem=rsem,
            device_id=(s_, to), device_id_type=MESH,
        )

    def own_copy(m, side):
        to = (x_right, x_left)[side]
        return weight_copy(x, mine + m, s, to, s_wx.at[side, m], r_wx.at[side, m])

    def far_copy(m):
        to = (x_right, x_left)[m]
        return weight_copy(around[m], mine + m, s, to, s_wf.at[m], r_wf.at[m])

    def line_copy(n, m):
        to = (s_up, s_down)[m]
        return weight_copy(around[n], mine + m, to, x, s_wy.at[n, m], r_wy.at[n, m])

    def share_mine(n, m):
        return weight_copy(around[n], mine + m, s + 1, x, s_ws.at[n, m], r_ws.at[n])

    def share_theirs(n, m):
        return weight_copy(around[n], theirs + m, s + 1, x, s_ws.at[n, 2 + m], r_ws.at[n])

    def take_theirs(n):
        for m in range(2):
            arrived(weight(around[n], theirs + m), r_wy.at[n, m])
            share_theirs(n, m).start()

    @pl.when(core0)
    def _():
        for m in range(2):
            own_copy(m, 0).start()
            own_copy(1 - m, 1).start()

    @pl.when(core1)
    def _():
        pl.semaphore_wait(barrier, 18)
        pl.semaphore_signal(go, inc=1, device_id=(s - 1, x), device_id_type=MESH)

    @pl.when(core0)
    def _():
        pl.semaphore_wait(go, 1)

    for h in range(4):
        for j in range(LOCAL_HEADS):
            cond = (y < 3) & ((g >= h) | (lower1 & (g + 1 == h))) & ((g != h) | (me != 2 * j + 1))
            send(cond, perm.at[j, 1:3, 0:16], rv.at[g, me], s_pv.at[h, j], r_v.at[g], line + 8 * h + 2 * j + 1)

    rv_sends = sends[-16:]
    for cond, copy in rv_sends:
        pl.when((g > 0) & cond)(copy.wait_send)
    sends[-16:] = [((g == 0) & cond, copy) for cond, copy in rv_sends]
    @pl.when((y < 3) & core1)
    def _():
        rv[g, me] = perm[i, 1:3, 0:16]

    for h in range(2):
        for j in range(LOCAL_HEADS):
            send(
                lower2, perm.at[j, 1:3, 0:32], r2.at[g, me], s_p2.at[h, j], r_2.at[g],
                line + 8 * (2 + h) + 2 * j + 1,
            )
    for j in range(LOCAL_HEADS):
        send(lower1, perm.at[j, 1:3, 0:64], r1.at[me], s_p1.at[j], r_1, base + 8 + 2 * j + 1)
    regroup(g >= 2, (1,))

    head = LOCAL_HEADS * x + i

    def send_back(b, lo):
        there = base + b
        pl.when(me != b)(
            pltpu.make_async_remote_copy(
                src_ref=ao.at[b], dst_ref=att.at[i, lo : lo + 64], send_sem=s_ret.at[b],
                recv_sem=r_att.at[i, lo // 64], device_id=(there, x), device_id_type=MESH,
            ).start
        )

        @pl.when(me == b)
        def _():
            att[i, lo : lo + 64] = ao[b]

    def wait_back(b, lo):
        pl.when(me != b)(
            pltpu.make_async_remote_copy(
                src_ref=ao.at[b], dst_ref=att.at[i, lo : lo + 64], send_sem=s_ret.at[b],
                recv_sem=r_att.at[i, lo // 64], device_id=(base + b, x), device_id_type=MESH,
            ).wait_send
        )

    @pl.when(core0)
    def _():
        blocks[me] = perm[i]

        def forward(b):
            return pltpu.make_async_remote_copy(
                src_ref=blocks.at[b, 0, 0:64], dst_ref=pre.at[b], send_sem=s_fwd.at[b], recv_sem=r_pre.at[b],
                device_id=(s + 1, x), device_id_type=MESH,
            )

        def hand(b):
            return pltpu.make_async_remote_copy(
                src_ref=stat.at[b], dst_ref=l0.at[b], send_sem=s_l0.at[b], recv_sem=r_l0.at[b],
                device_id=(s + 1, x), device_id_type=MESH,
            )

        for side in range(2):
            m = side
            arrived(weight(around[side], mine + m), r_wx.at[side, m])
            far_copy(m).start()
            line_copy(side, m).start()
            share_mine(side, m).start()

        for b in range(8):
            pl.when(me != b)(functools.partial(arrived, blocks.at[b, :, 0:64], r_blk.at[0, b]))
            forward(b).start()
        for side in range(2):
            m = 1 - side
            arrived(weight(around[side], mine + m), r_wx.at[side, m])
            line_copy(side, m).start()
            share_mine(side, m).start()

        for m in range(2):
            arrived(weight(x_far, mine + m), r_wf.at[m])
            line_copy(2, m).start()
            share_mine(2, m).start()
        same = position(lane, head) <= position(row, head)
        times = (1 + jnp.minimum(levels(row), levels(lane))).astype(F32)
        half = lax.broadcasted_iota(jnp.int32, (64, ROWS), 1) < 64
        for b in range(8):
            pl.when(me != b)(functools.partial(arrived, blocks.at[b, :, 64:128], r_blk.at[1, b]))
            width = ROWS * (b + 1)
            keys = blocks[0 : b + 1, 1].reshape(width, HEAD_DIM)
            values = blocks[0 : b + 1, 2].reshape(width, HEAD_DIM)
            scores = dot_t(blocks[b, 0], keys) * SCALE
            last = jnp.where(same, scores[:, ROWS * b :], NEG)
            scores = last if b == 0 else jnp.concatenate([scores[:, : ROWS * b], last], axis=1)
            peak = jnp.max(scores, axis=1, keepdims=True)
            weights = jnp.exp2(scores - peak) * jnp.concatenate([times] * (b + 1), axis=1)
            total = jnp.sum(weights, axis=1, keepdims=True)
            numer = dot(weights.astype(BF16), values)
            stat[b, 0] = numer[:64]
            stat[b, 1] = jnp.where(half, peak[:64], total[:64])
            hand(b).start()
            ao[b] = (numer[64:] / total[64:]).astype(BF16)
            send_back(b, 64)
        take_theirs(0)
        take_theirs(1)
        pl.when(g == 0)(functools.partial(take_theirs, 2))

        for b in range(8):
            forward(b).wait_send()
            hand(b).wait_send()
            wait_back(b, 64)

    @pl.when(core1)
    def _():
        def arrived_if(cond, ref, sem):
            pl.when(cond)(functools.partial(arrived, ref, sem))

        passes = []

        def pass_on(cond, h, src):
            def to_line(where, d, src, dst, rsem):
                copy = pltpu.make_async_remote_copy(
                    src_ref=src, dst_ref=dst, send_sem=s_y.at[d - 1, h], recv_sem=rsem,
                    device_id=(s + 32 * d, x), device_id_type=MESH,
                )
                pl.when(cond & where)(copy.start)
                passes.append((cond & where, copy))

            to_line(lax.rem(y, 2) == 0, 1, src, ry.at[h], r_y.at[2])

            @pl.when(cond & (y < 2))
            def _():
                rows = src[...].astype(F32)
                pack[h] = jnp.concatenate([rows[:, 0, 0:8], rows[:, 1, 0:8]], axis=1).astype(BF16)

            to_line(y == 0, 3, pack.at[h], rp.at[0, h], r_y.at[0])
            to_line(y == 0, 2, pack.at[h], rp.at[0, h], r_y.at[0])
            to_line(y == 1, 1, pack.at[h], rp.at[1, h], r_y.at[1])
            to_line(y == 1, 2, pack.at[h], rp.at[1, h], r_y.at[1])

        for h in range(4):
            later = (y < 3) & ((g <= h) | (upper1 & (g == h + 1)))
            arrived_if(later & (g != h), rv.at[h], r_v.at[h])
            arrived_if(later & (g == h), rv.at[h, 0:7], r_v.at[h])
            pass_on(later, h, rv.at[h])
        for h in range(2):
            arrived_if(upper2, r2.at[h], r_2.at[h])
            pass_on(upper2, h, r2.at[h, :, :, 0:16])

        for b in range(8):
            arrived(pre.at[b], r_pre.at[b])

        top[...] = jnp.full_like(top, NEG)
        den[...] = jnp.zeros_like(den)
        num[...] = jnp.zeros_like(num)

        def update(w, keys, values, packed=False):
            nb = ROWS // w
            shape = (ROWS, keys.shape[0])
            r_query = lax.rem(lax.broadcasted_iota(jnp.int32, shape, 0), w)
            r_key = lax.rem(lax.broadcasted_iota(jnp.int32, shape, 1), w)
            if packed:
                both = (r_query < 8) & (r_key < 8)
                count = jnp.where(both, 1.0, 0.0)
            else:
                count = (jnp.minimum(levels(r_query), levels(r_key)) - {64: 0, 32: 1, 16: 2}[w]).astype(F32)
            for b0 in range(0, 8, nb):
                at = (slice(b0, b0 + nb), slice(0, w))
                query = pre[b0 : b0 + nb, 0:w].reshape(ROWS, HEAD_DIM)
                scores = dot_t(query, keys) * SCALE
                if packed:
                    scores = jnp.where(both, scores, NEG)
                was = top[at].reshape(ROWS, HEAD_DIM)
                peak = jnp.maximum(was, jnp.max(scores, axis=1, keepdims=True))
                keep = jnp.exp2(was - peak)
                weights = jnp.exp2(scores - peak[:, :1]) * count
                total = jnp.sum(weights, axis=1, keepdims=True) + den[at].reshape(ROWS, HEAD_DIM) * keep
                if packed:
                    weights = pltpu.roll(weights, 8, axis=1)
                numer = dot(weights.astype(BF16), values) + num[at].reshape(ROWS, HEAD_DIM) * keep
                top[at] = peak.reshape(nb, w, HEAD_DIM)
                den[at] = total.reshape(nb, w, HEAD_DIM)
                num[at] = numer.reshape(nb, w, HEAD_DIM)

        def level_rows(ref, n, w, rows):
            return ref[..., n, 0:w, :].reshape(rows, HEAD_DIM)

        @pl.when(upper2)
        def _():
            update(32, level_rows(r2, 0, 32, 512), level_rows(r2, 1, 32, 512))

        arrived_if(upper1, r1, r_1)

        @pl.when(upper1)
        def _():
            update(64, level_rows(r1, 0, 64, 512), level_rows(r1, 1, 64, 512))

        @pl.when(y >= 2)
        def _():
            for t in range(2):
                arrived(rp.at[t], r_y.at[t])
            tiles = rp[...].reshape(1024, HEAD_DIM)
            update(16, tiles, tiles, packed=True)

        @pl.when(lax.rem(y, 2) == 1)
        def _():
            arrived(ry, r_y.at[2])
            update(16, ry[:, :, 0].reshape(512, HEAD_DIM), ry[:, :, 1].reshape(512, HEAD_DIM))

        for b in range(8):
            arrived(l0.at[b], r_l0.at[b])
            peak, total = l0[b, 1, :, 0:1], l0[b, 1, :, 64:65]
            was = top[b]
            best = jnp.maximum(was, peak)
            keep, gain = jnp.exp2(was - best), jnp.exp2(peak - best)
            numer = num[b] * keep + l0[b, 0] * gain
            total = den[b] * keep + total * gain
            ao[b] = (numer / total).astype(BF16)
            send_back(b, 0)
        for b in range(8):
            wait_back(b, 0)

        for cond, copy in passes:
            pl.when(cond)(copy.wait_send)

    def quarter(x_):
        return pl.ds(pl.multiple_of(32 * x_, 32), 32)

    for j in range(LOCAL_HEADS):
        for half in range(2):
            sender = 2 * j + (1 - half)
            pl.when(me != sender)(
                functools.partial(arrived, att.at[j, 64 * half : 64 * half + 64], r_att.at[j, half])
            )
        pick = jnp.where(row == position(lane, LOCAL_HEADS * x + j), 1.0, 0.0).astype(BF16)
        nat[j] = dot(pick, att[j]).astype(BF16)
        for d in (2, 1, 3):
            there = lax.rem(x + d, X)
            send(None, nat.at[j, quarter(there)], ax.at[x, j], s_ax.at[d - 1, j], r_ax.at[d - 1], s, there)

    pl.when(core0 & (g > 0))(functools.partial(take_theirs, 2))

    for d in (0, 1, 3, 2):
        there = lax.rem(x + X - d, X)
        if d == 0:
            rows = nat[:, quarter(x)]
        else:
            arrived(ax.at[there], r_ax.at[d - 1])
            rows = ax[there]
            n = {1: 0, 3: 1, 2: 2}[d]
            pl.when(core1)(functools.partial(arrived, w_ref.at[there], r_ws.at[n]))
        rows = jnp.concatenate([rows[j] for j in range(LOCAL_HEADS)], axis=1)
        for n in range(D // COLS):
            cols = slice(n * COLS, (n + 1) * COLS)
            product = dot(rows, w_ref[there, :, cols])
            if d > 0:
                product = product + part[:, cols]
            if d == 2:
                o_ref[:, cols] = product.astype(BF16)
            else:
                part[:, cols] = product
    @pl.when(core0)
    def _():
        for m in range(2):
            own_copy(m, 0).wait_send()
            own_copy(m, 1).wait_send()
            far_copy(m).wait_send()
            for n in range(3):
                line_copy(n, m).wait_send()
                share_mine(n, m).wait_send()
                share_theirs(n, m).wait_send()

    for cond, copy in sends:
        if cond is None:
            copy.wait_send()
        else:
            pl.when(cond)(copy.wait_send)

def per_device(query_rows, key_rows, value_rows, out_weight):
    vmem = pl.BlockSpec(memory_space=pltpu.VMEM)
    dma = pltpu.SemaphoreType.DMA
    hd = HEAD_DIM
    return pl.pallas_call(
        kernel,
        out_shape=jax.ShapeDtypeStruct((ROWS // X, D), BF16),
        in_specs=[pl.BlockSpec(memory_space=pl.ANY)] * 4,
        out_specs=vmem,
        scratch_shapes=[
            pltpu.VMEM((ROWS, LOCAL_HEADS * hd), BF16),
            pltpu.VMEM((ROWS, LOCAL_HEADS * hd), BF16),
            pltpu.VMEM((ROWS, LOCAL_HEADS * hd), BF16),
            pltpu.VMEM((LOCAL_HEADS, 3, ROWS, hd), BF16),
            pltpu.VMEM((8, 3, ROWS, hd), BF16),
            pltpu.VMEM((8, 64, hd), BF16),
            pltpu.VMEM((8, 2, 64, hd), BF16),
            pltpu.VMEM((2, 8, 2, 32, hd), BF16),
            pltpu.VMEM((4, 8, 2, 16, hd), BF16),
            pltpu.VMEM((4, 8, 2, 16, hd), BF16),
            pltpu.VMEM((2, 4, 8, 16, hd), BF16),
            pltpu.VMEM((4, 8, 16, hd), BF16),
            pltpu.VMEM((8, 2, 64, hd), F32),
            pltpu.VMEM((8, 2, 64, hd), F32),
            pltpu.VMEM((8, 64, hd), F32),
            pltpu.VMEM((8, 64, hd), F32),
            pltpu.VMEM((8, 64, hd), F32),
            pltpu.VMEM((8, 64, hd), BF16),
            pltpu.VMEM((LOCAL_HEADS, ROWS, hd), BF16),
            pltpu.VMEM((LOCAL_HEADS, ROWS, hd), BF16),
            pltpu.VMEM((X, LOCAL_HEADS, ROWS // X, hd), BF16),
            pltpu.VMEM((X, LOCAL_HEADS * hd, D), BF16),
            pltpu.VMEM((ROWS // X, D), F32),
            pltpu.SemaphoreType.REGULAR,
            dma((3,)), dma, dma((4,)), dma((2, 4)), dma((4, 4)), dma((2, 4)), dma((8,)), dma((3, 4)),
            dma((8,)), dma((8,)), dma((X - 1, 4)), dma((2, 2)), dma((2,)), dma((3, 2)), dma((3, 4)),
            dma((2, 8)), dma((8,)), dma, dma((2,)), dma((4,)), dma((3,)), dma((8,)), dma((4, 2)),
            dma((X - 1,)), dma((2, 2)), dma((2,)), dma((3, 2)), dma((3,)),
        ],
        compiler_params=pltpu.CompilerParams(
            collective_id=0, has_side_effects=True, vmem_limit_bytes=60 * 1024 * 1024
        ),
    )(query_rows, key_rows, value_rows, out_weight)

def solution(mesh):
    in_specs = (P("seq", "head"), P("seq", "head"), P("seq", "head"), P("head", None))
    return jax.shard_map(
        per_device, mesh=mesh, in_specs=in_specs, out_specs=P(("seq", "head"), None), check_vma=False
    )
```
